256 devices in a mesh: dp: 8 (over z), expert: 32 (over x, y, core).
Axes of the slice: x: 4, y: 4, z: 8, core: 2. Of those that a mesh axis runs over, the one named last changes fastest.
Arguments:
- tokens: bfloat16 [32768, 2048], P(('dp', 'expert')), may hold values from -6 to 6
- grad_out: bfloat16 [32768, 2048], P(('dp', 'expert')), may hold values from -24 to 24
- gates: float32 [32768, 8], P(('dp', 'expert')), may hold values from 0.05 to 0.5
- expert_ids: int32 [32768, 8], P(('dp', 'expert')), may hold values from 0 to 31, all different within a row; in each aligned block of 128 rows (0 to 127, 128 to 255, ...) at most 36 rows name the same one
- w_gate: bfloat16 [32, 2048, 384], P('expert'), may hold values from -0.125 to 0.125
- w_up: bfloat16 [32, 2048, 384], P('expert'), may hold values from -0.125 to 0.125
- w_down: bfloat16 [32, 384, 2048], P('expert'), may hold values from -0.3125 to 0.3125
Outputs:
- grad_tokens: bfloat16 [32768, 2048], P(('dp', 'expert'))
- grad_gate: bfloat16 [32, 2048, 384], P('expert', 'dp')
- grad_up: bfloat16 [32, 2048, 384], P('expert', 'dp')
- grad_down: bfloat16 [32, 384, 2048], P('expert', 'dp')
The draws below stay inside these ranges and needn't reach their ends.
Inputs may be any that keep to these rules, and one draw needn't show every extreme that they name: `expert_ids`: each row names 8 different experts. In the rows of one device no expert is named more than 36 times, a bound that some block reaches.
All inputs are finite; a program needn't handle non-finite values.
Results may differ from the reference program's by a relative error of at most 0.019.
Values may be sent and summed in bfloat16 or wider, within the bound.
No kernel may reach another device: no remote copies, remote signals or barrier semaphores. Data moves between devices by JAX's collectives and lax.ppermute only.
A program may use at most 128 MiB of HBM per device.

```python
import math
import jax
import jax.numpy as jnp
import numpy as np
from jax import lax

D = 2048
FF = 384
TOP = 8
TOK_DEV = 128
EXPERTS = 32
TOKENS = 32768
MOST = 36
DEVICES = 256


def block_levels(key, shape, cuts, smallest, high):
    def one(axis_at, shards_of):
        heights = jax.random.uniform(jax.random.fold_in(jax.random.fold_in(key, 6), axis_at), (shards_of,), jnp.float32, smallest / len(cuts), high / len(cuts))
        return jnp.repeat(jnp.exp(heights), shape[axis_at] // shards_of).reshape((-1,) + (1,) * (len(shape) - axis_at - 1))

    loudness = one(*cuts[0])
    for cut in cuts[1:]:
        loudness = loudness * one(*cut)
    return loudness


def shared_out(stream_key, own, number, rows, amount, top, reach, lean):
    order = jax.random.permutation(stream_key, amount)
    crowded, usual = shares(amount, rows * top, reach, lean, True), shares(amount, rows * top, reach, lean, False)
    places = jnp.arange(amount)

    def named(sizes, turn):
        used = int((sizes > 0).sum())
        fixed = max(1, used // 4)
        shifted = fixed + (places - fixed + turn * (used - fixed)) % max(1, amount - fixed)
        return jnp.zeros((amount,), jnp.int32).at[order[jnp.where(places < fixed, places, shifted)]].set(jnp.asarray(sizes, jnp.int32))

    sizes = jnp.where(number % 4 == 0, named(crowded, number // 4), named(usual, number - number // 4 - 1))
    mixed = jax.random.permutation(jax.random.fold_in(own, 3), amount)
    donor, sink = mixed[0:amount // 2 * 2:2], mixed[1:amount // 2 * 2:2]
    margin = jnp.minimum(sizes[donor] - 1, reach - sizes[sink]) // 2
    margin = jnp.where((donor == order[0]) | (sink == order[0]) | (sizes[sink] == 0), 0, jnp.maximum(margin, 0))
    shifted = jax.random.randint(jax.random.fold_in(own, 4), (amount // 2,), 0, 1 << 20) % (margin + 1)
    sizes = sizes.at[donor].add(-shifted).at[sink].add(shifted)
    members = jnp.searchsorted(jnp.cumsum(sizes), jnp.arange(rows * top), side="right").astype(jnp.int32)
    listing = members.reshape(top, rows).T
    listing = listing[jax.random.permutation(jax.random.fold_in(own, 1), rows)]
    turn = jax.random.randint(jax.random.fold_in(own, 2), (rows, 1), 0, top)
    return jnp.take_along_axis(listing, (jnp.arange(top)[None, :] + turn) % top, axis=1)


def shares(count, total, reach, lean, full):
    loads = [(1 << 20) // math.isqrt(grade ** lean) + 1 for grade in range(1, count + 1)]
    largest = reach if full else min(reach, max(-(-total // count), total * loads[0] // sum(loads)))
    least = 1 if total - largest >= count - 1 else 0
    counts, surplus = [largest] + [least] * (count - 1), total - largest - least * (count - 1)
    while surplus > 0:
        free = [i for i in range(1, count) if counts[i] < largest] or [i for i in range(1, count) if counts[i] < reach]
        pool, budget = sum([loads[i] for i in free]), surplus
        for i in free:
            addition = min(reach - counts[i], max(1, budget * loads[i] // pool), surplus)
            counts[i] = counts[i] + addition
            surplus = surplus - addition
    return np.array(counts)


def normal_values(rng, shape, spread, bound, split=(), kind=jnp.bfloat16):
    array = jax.random.normal(rng, shape, jnp.float32) * spread
    if len(split) > 0:
        array = block_levels(rng, shape, split, -0.22, 0.18) * array
    return jnp.clip(array, min=-bound, max=bound).astype(kind)


def setup_inputs(seed: int = 0) -> dict:
    key_list = jax.random.split(jax.random.key(seed), 8)
    tokens = normal_values(key_list[0], (TOKENS, D), 1.0, 6.0, ((0, 256),))
    grad_out = normal_values(key_list[1], (TOKENS, D), 4.0, 24.0, ((0, 256),))
    gates = jnp.clip(jnp.exp(math.log(0.5) - 2.3025851 * jax.random.uniform(key_list[2], (TOKENS, TOP), jnp.float32) ** block_levels(key_list[2], (TOKENS, TOP), ((0, 256),), -0.2, 0.2)), 0.05, 0.5)
    expert_ids_keys = jax.random.split(jax.random.fold_in(key_list[3], 1), TOKENS // TOK_DEV)
    expert_ids_turns = jax.random.permutation(jax.random.fold_in(key_list[3], 3), TOKENS // TOK_DEV)
    expert_ids = jax.vmap(lambda own, number: shared_out(jax.random.fold_in(key_list[3], 2), own, number, TOK_DEV, EXPERTS, TOP, MOST, 1))(expert_ids_keys, expert_ids_turns).reshape((TOKENS, TOP))
    w_gate = normal_values(key_list[4], (EXPERTS, D, FF), D ** -0.5, 0.125, ((0, 32),))
    w_up = normal_values(key_list[5], (EXPERTS, D, FF), D ** -0.5, 0.125, ((0, 32),))
    w_down = normal_values(key_list[6], (EXPERTS, FF, D), FF ** -0.5, 0.3125, ((0, 32),))
    return dict(tokens=tokens, grad_out=grad_out, gates=gates, expert_ids=expert_ids, w_gate=w_gate, w_up=w_up, w_down=w_down)


def expert_backward(rows_x, routed, wg, wu, wd):
    pre_gate = jnp.dot(rows_x, wg, preferred_element_type=jnp.float32)
    pre_up = jnp.dot(rows_x, wu, preferred_element_type=jnp.float32)
    sigma = jax.nn.sigmoid(pre_gate)
    silu_part = pre_gate * sigma
    act = (silu_part * pre_up).astype(jnp.bfloat16)
    d_act = jnp.dot(routed, wd.T, preferred_element_type=jnp.float32)
    d_gate = (d_act * pre_up * sigma * (1.0 + pre_gate * (1.0 - sigma))).astype(jnp.bfloat16)
    d_up = (d_act * silu_part).astype(jnp.bfloat16)
    summed = jnp.dot(d_gate, wg.T, preferred_element_type=jnp.float32) + jnp.dot(d_up, wu.T, preferred_element_type=jnp.float32)
    return act, d_gate, d_up, summed.astype(jnp.bfloat16)


def reference(tokens, grad_out, gates, expert_ids, w_gate, w_up, w_down):
    pairs = TOKENS * TOP
    capacity = DEVICES * MOST
    flat_ids = expert_ids.reshape(-1)
    flat_gates = gates.reshape(-1)

    def one_expert(accum, inputs):
        ident, wg, wu, wd = inputs
        (picked,) = jnp.nonzero(flat_ids == ident, size=capacity, fill_value=pairs)
        picked = picked.astype(jnp.int32)
        owners = (picked // TOP).astype(jnp.int32)
        rows_x = jnp.take(tokens, owners, axis=0, mode="fill", fill_value=0)
        weights = jnp.take(flat_gates, picked, mode="fill", fill_value=0)
        rows_dy = jnp.take(grad_out, owners, axis=0, mode="fill", fill_value=0).astype(jnp.float32)
        routed = (weights[:, None] * rows_dy).astype(jnp.bfloat16)
        act, d_gate, d_up, pair_grad = expert_backward(rows_x, routed, wg, wu, wd)
        accum = accum.at[owners].add(pair_grad.astype(jnp.float32), mode="drop")
        grad_g = jnp.dot(rows_x.T, d_gate, preferred_element_type=jnp.float32).astype(jnp.bfloat16)
        grad_u = jnp.dot(rows_x.T, d_up, preferred_element_type=jnp.float32).astype(jnp.bfloat16)
        grad_d = jnp.dot(act.T, routed, preferred_element_type=jnp.float32).astype(jnp.bfloat16)
        return accum, (grad_g, grad_u, grad_d)

    start = jnp.zeros((TOKENS, D), jnp.float32)
    idents = jnp.arange(EXPERTS, dtype=jnp.int32)
    accum, (grad_gate, grad_up, grad_down) = lax.scan(one_expert, start, (idents, w_gate, w_up, w_down))
    return accum.astype(jnp.bfloat16), grad_gate, grad_up, grad_down
```

```python
import functools

import jax
import jax.numpy as jnp
from jax import lax
from jax.experimental import pallas as pl
from jax.experimental.pallas import tpu as pltpu
from jax.sharding import PartitionSpec as P

BF = jnp.bfloat16
F32 = jnp.float32
MIB = 1 << 20

MAIN = 32
REM = 4
PACK = 2 * (MAIN + REM)


def dot(a, b, ca=1, cb=0):
    return lax.dot_general(a, b, (((ca,), (cb,)), ((), ())), preferred_element_type=F32)


def iota(shape, dim):
    return lax.broadcasted_iota(jnp.int32, shape, dim)


def positions(ids, experts):
    toks, top = ids.shape
    ids_t = ids.astype(F32).T
    ident = iota((experts, toks), 0).astype(F32)
    member = jnp.zeros((experts, toks), F32)
    for k in range(top):
        member = member + jnp.where(ids_t[k : k + 1, :] == ident, 1.0, 0.0)
    before = (iota((toks, toks), 0) < iota((toks, toks), 1)).astype(F32).astype(BF)
    pos = dot(member.astype(BF), before)
    return jnp.where(member > 0.5, pos, -1.0), ids_t, ident


def select(pos):
    experts, toks = pos.shape
    wide = pos[:, None, :]
    main = (wide == iota((experts, MAIN, toks), 1).astype(F32)).astype(F32)
    rest = (wide == (MAIN + iota((experts, 2 * REM, toks), 1) % REM).astype(F32)).astype(F32)
    return main.reshape(experts * MAIN, toks), rest.reshape(experts * 2 * REM, toks)


def is_left(rows, cols):
    return iota((rows, cols), 0) % (2 * REM) < REM


def dispatch_kernel(scaled, *refs):
    if scaled:
        ids_ref, gates_ref, left_ref, right_ref, out_ref, main_ref, rest_ref, gmain_ref, grest_ref = refs
    else:
        ids_ref, left_ref, right_ref, out_ref, main_ref, rest_ref = refs
    experts, _, width = out_ref.shape

    @pl.when(pl.program_id(0) == 0)
    def _():
        pos, ids_t, ident = positions(ids_ref[...], experts)
        main, rest = select(pos)
        main_ref[...] = main.astype(BF)
        rest_ref[...] = rest.astype(BF)
        if scaled:
            gates_t = gates_ref[...].T
            weight = jnp.zeros(pos.shape, F32)
            for k in range(gates_t.shape[0]):
                weight = weight + jnp.where(ids_t[k : k + 1, :] == ident, gates_t[k : k + 1, :], 0.0)
            toks = pos.shape[1]
            for rows, sel, ref in ((MAIN, main, gmain_ref), (2 * REM, rest, grest_ref)):
                wide = jnp.broadcast_to(weight[:, None, :], (experts, rows, toks)).reshape(experts * rows, toks)
                ref[...] = jnp.broadcast_to(jnp.sum(sel * wide, axis=1, keepdims=True), ref.shape)

    left, right = left_ref[...], right_ref[...]

    def rows_of(sel_ref, g_ref, data):
        got = dot(sel_ref[...], data)
        if scaled:
            got = got * jnp.concatenate([g_ref[...]] * (width // 128), axis=1)
        return got

    gm = gmain_ref if scaled else None
    gr = grest_ref if scaled else None
    out_ref[:, 0:MAIN, :] = rows_of(main_ref, gm, left).astype(BF).reshape(experts, MAIN, width)
    out_ref[:, MAIN : 2 * MAIN, :] = rows_of(main_ref, gm, right).astype(BF).reshape(experts, MAIN, width)
    rest_l = rows_of(rest_ref, gr, left)
    rest_r = rows_of(rest_ref, gr, right)
    both = jnp.where(is_left(*rest_l.shape), rest_l, rest_r)
    out_ref[:, 2 * MAIN : PACK, :] = both.astype(BF).reshape(experts, 2 * REM, width)


def dispatch(ids, data, experts, gates=None):
    toks, width = data.shape
    half, steps = width // 2, 4
    cols = half // steps
    full = lambda a: pl.BlockSpec(a.shape, lambda c: (0,) * a.ndim)
    small = [ids] if gates is None else [ids, gates]
    scratch = [pltpu.VMEM((experts * MAIN, toks), BF), pltpu.VMEM((experts * 2 * REM, toks), BF)]
    if gates is not None:
        scratch += [pltpu.VMEM((experts * MAIN, 128), F32), pltpu.VMEM((experts * 2 * REM, 128), F32)]
    return pl.pallas_call(
        functools.partial(dispatch_kernel, gates is not None),
        out_shape=jax.ShapeDtypeStruct((experts, PACK, half), BF),
        grid=(steps,),
        in_specs=[full(a) for a in small]
        + [pl.BlockSpec((toks, cols), lambda c: (0, c)), pl.BlockSpec((toks, cols), lambda c: (0, c + steps))],
        out_specs=pl.BlockSpec((experts, PACK, cols), lambda c: (0, 0, c)),
        scratch_shapes=scratch,
        compiler_params=pltpu.CompilerParams(vmem_limit_bytes=28 * MIB),
        cost_estimate=pl.CostEstimate(flops=2 * 1280 * toks * width, bytes_accessed=6 * MIB, transcendentals=0),
        name="dispatch",
    )(*small, data, data)


def halves(ref):
    n, _, half = ref.shape
    rest = ref[:, 2 * MAIN : PACK, :].reshape(n * 2 * REM, half)
    left = ref[:, 0:MAIN, :].reshape(n * MAIN, half)
    right = ref[:, MAIN : 2 * MAIN, :].reshape(n * MAIN, half)
    return jnp.concatenate([left, rest], axis=0), jnp.concatenate([right, rest], axis=0)


def joined(p_left, p_right, mains):
    main = p_left[:mains] + p_right[:mains]
    tail = p_right[mains:]
    rest = p_left[mains:] + pltpu.roll(tail, tail.shape[0] - REM, 0)
    return main, jnp.where(is_left(*rest.shape), rest, 0.0)


def forward_kernel(x_ref, wg_ref, wu_ref, csm_ref, csr_ref, actm_ref, actr_ref, wcat_ref):
    hidden = wg_ref.shape[1]
    half = x_ref.shape[2]

    @pl.when(pl.program_id(0) == 0)
    def _():
        wcat_ref[:, :hidden] = wg_ref[...]
        wcat_ref[:, hidden:] = wu_ref[...]

    mains = x_ref.shape[0] * MAIN
    a_left, a_right = halves(x_ref)
    pre = joined(dot(a_left, wcat_ref[:half, :]), dot(a_right, wcat_ref[half:, :]), mains)
    for p, cs_ref, act_ref in zip(pre, (csm_ref, csr_ref), (actm_ref, actr_ref)):
        gate, up = p[:, :hidden], p[:, hidden:]
        sigma = jax.nn.sigmoid(gate)
        silu = gate * sigma
        cs_ref[:, :hidden] = up * sigma * (1.0 + gate * (1.0 - sigma))
        cs_ref[:, hidden:] = silu
        act_ref[...] = (silu * up).astype(BF)


def forward(rx, wg, wu):
    n, _, half = rx.shape
    width, hidden = wg.shape
    steps = 4
    step = n // steps
    rows = lambda per, cols: pl.BlockSpec((step * per, cols), lambda i: (i, 0))
    full = lambda shape: pl.BlockSpec(shape, lambda i: (0, 0))
    mains, rests = n * MAIN, n * 2 * REM
    return pl.pallas_call(
        forward_kernel,
        out_shape=(
            jax.ShapeDtypeStruct((mains, 2 * hidden), F32),
            jax.ShapeDtypeStruct((rests, 2 * hidden), F32),
            jax.ShapeDtypeStruct((mains, hidden), BF),
            jax.ShapeDtypeStruct((rests, hidden), BF),
            jax.ShapeDtypeStruct((width, 2 * hidden), BF),
        ),
        grid=(steps,),
        in_specs=[
            pl.BlockSpec((step, PACK, half), lambda i: (i, 0, 0)),
            full((width, hidden)),
            full((width, hidden)),
        ],
        out_specs=(
            rows(MAIN, 2 * hidden),
            rows(2 * REM, 2 * hidden),
            rows(MAIN, hidden),
            rows(2 * REM, hidden),
            full((width, 2 * hidden)),
        ),
        compiler_params=pltpu.CompilerParams(vmem_limit_bytes=40 * MIB),
        cost_estimate=pl.CostEstimate(
            flops=2 * (mains + rests) * width * 2 * hidden, bytes_accessed=16 * MIB, transcendentals=mains * hidden
        ),
        name="forward",
    )(rx, wg, wu)


def hidden_grad_kernel(g_ref, wd_ref, csm_ref, csr_ref, dm_ref, dr_ref):
    half = g_ref.shape[2]
    mains = g_ref.shape[0] * MAIN
    a_left, a_right = halves(g_ref)
    d_act = joined(dot(a_left, wd_ref[:, :half], 1, 1), dot(a_right, wd_ref[:, half:], 1, 1), mains)
    for d, cs_ref, out_ref in zip(d_act, (csm_ref, csr_ref), (dm_ref, dr_ref)):
        out_ref[...] = (jnp.concatenate([d, d], axis=1) * cs_ref[...]).astype(BF)


def hidden_grad(rg, wd, csm, csr):
    n, _, half = rg.shape
    hidden = wd.shape[0]
    steps = 4
    step = n // steps
    rows = lambda per, cols: pl.BlockSpec((step * per, cols), lambda i: (i, 0))
    mains, rests = n * MAIN, n * 2 * REM
    return pl.pallas_call(
        hidden_grad_kernel,
        out_shape=(
            jax.ShapeDtypeStruct((mains, 2 * hidden), BF),
            jax.ShapeDtypeStruct((rests, 2 * hidden), BF),
        ),
        grid=(steps,),
        in_specs=[
            pl.BlockSpec((step, PACK, half), lambda i: (i, 0, 0)),
            pl.BlockSpec(wd.shape, lambda i: (0, 0)),
            rows(MAIN, 2 * hidden),
            rows(2 * REM, 2 * hidden),
        ],
        out_specs=(rows(MAIN, 2 * hidden), rows(2 * REM, 2 * hidden)),
        compiler_params=pltpu.CompilerParams(vmem_limit_bytes=32 * MIB),
        cost_estimate=pl.CostEstimate(
            flops=2 * (mains + rests) * 2 * half * hidden, bytes_accessed=12 * MIB, transcendentals=0
        ),
        name="hidden_grad",
    )(rg, wd, csm, csr)


def shifted(rest):
    return pltpu.roll(rest.astype(F32), REM, 0)


def weight_grad_kernel(x_ref, g_ref, dm_ref, dr_ref, actm_ref, actr_ref, out_ref, dt_ref, at_ref):
    copies = out_ref.shape[0]
    n, _, half = x_ref.shape
    mains = n * MAIN
    both, hidden = dm_ref.shape[1], actm_ref.shape[1]

    for src_m, src_r, dst in ((dm_ref, dr_ref, dt_ref), (actm_ref, actr_ref, at_ref)):
        main_t = src_m[...].T
        rest = src_r[...]
        dst[0, :, :mains] = main_t
        dst[1, :, :mains] = main_t
        dst[0, :, mains:] = rest.T
        dst[1, :, mains:] = shifted(rest).astype(BF).T

    tile = 256
    per = 2 * half // copies
    slab = hidden // copies
    base = both * per // 128
    for side in range(2):
        for j in range(half // tile):
            cols = pl.ds(j * tile, tile)

            def rows_of(ref):
                main = ref[:, side * MAIN : (side + 1) * MAIN, cols].reshape(mains, tile)
                rest = ref[:, 2 * MAIN : PACK, cols].reshape(n * 2 * REM, tile)
                return jnp.concatenate([main, rest], axis=0)

            into = dot(dt_ref[side], rows_of(x_ref)).astype(BF)
            down = dot(at_ref[side], rows_of(g_ref)).astype(BF)
            for q in range(tile // 128):
                at = (side * half + j * tile) // 128 + q
                owner, piece = at * 128 // per, at % (per // 128)
                part = into[:, q * 128 : (q + 1) * 128]
                out_ref[owner, piece * both : (piece + 1) * both, :] = part
                part = down[:, q * 128 : (q + 1) * 128].reshape(copies, slab, 128)
                out_ref[:, base + at * slab : base + (at + 1) * slab, :] = part


def weight_grad(rx, rg, dm, dr, actm, actr, copies):
    n, _, half = rx.shape
    both, hidden = dm.shape[1], actm.shape[1]
    rows = dm.shape[0] + dr.shape[0]
    length = 3 * hidden * 2 * half // copies // 128
    return pl.pallas_call(
        weight_grad_kernel,
        out_shape=jax.ShapeDtypeStruct((copies, length, 128), BF),
        in_specs=[pl.BlockSpec(memory_space=pltpu.VMEM)] * 6,
        out_specs=pl.BlockSpec(memory_space=pltpu.VMEM),
        scratch_shapes=[pltpu.VMEM((2, both, rows), BF), pltpu.VMEM((2, hidden, rows), BF)],
        compiler_params=pltpu.CompilerParams(vmem_limit_bytes=40 * MIB),
        cost_estimate=pl.CostEstimate(
            flops=2 * rows * 2 * half * 3 * hidden, bytes_accessed=18 * MIB, transcendentals=0
        ),
        name="weight_grad",
    )(rx, rg, dm, dr, actm, actr)


def unpack_kernel(in_ref, gate_ref, up_ref, down_ref):
    per, hidden = gate_ref.shape
    slab = down_ref.shape[0]
    base = 2 * hidden * per // 128
    for q in range(per // 128):
        both = in_ref[q * 2 * hidden : (q + 1) * 2 * hidden, :].T
        gate_ref[q * 128 : (q + 1) * 128, :] = both[:, :hidden]
        up_ref[q * 128 : (q + 1) * 128, :] = both[:, hidden:]
    for q in range(down_ref.shape[1] // 128):
        down_ref[:, q * 128 : (q + 1) * 128] = in_ref[base + q * slab : base + (q + 1) * slab, :]


def unpack(summed, per, hidden, width, slab):
    vmem = pl.BlockSpec(memory_space=pltpu.VMEM)
    return pl.pallas_call(
        unpack_kernel,
        out_shape=(
            jax.ShapeDtypeStruct((per, hidden), BF),
            jax.ShapeDtypeStruct((per, hidden), BF),
            jax.ShapeDtypeStruct((slab, width), BF),
        ),
        in_specs=[vmem],
        out_specs=(vmem, vmem, vmem),
        cost_estimate=pl.CostEstimate(flops=0, bytes_accessed=2 * MIB, transcendentals=0),
        name="unpack",
    )(summed)


def pair_grad_kernel(dm_ref, dr_ref, wcat_ref, out_ref):
    n, _, half = out_ref.shape
    mains = n * MAIN
    main, rest = dm_ref[...], dr_ref[...]
    d_left = jnp.concatenate([main, rest], axis=0)
    d_right = jnp.concatenate([main, shifted(rest).astype(BF)], axis=0)
    y_left = dot(d_left, wcat_ref[:half, :], 1, 1)
    y_right = dot(d_right, wcat_ref[half:, :], 1, 1)
    out_ref[:, 0:MAIN, :] = y_left[:mains].astype(BF).reshape(n, MAIN, half)
    out_ref[:, MAIN : 2 * MAIN, :] = y_right[:mains].astype(BF).reshape(n, MAIN, half)
    out_ref[:, 2 * MAIN : PACK, :] = (y_left[mains:] + y_right[mains:]).astype(BF).reshape(n, 2 * REM, half)


def pair_grad(dm, dr, wcat):
    width, both = wcat.shape
    n, half = dm.shape[0] // MAIN, width // 2
    steps = 4
    step = n // steps
    return pl.pallas_call(
        pair_grad_kernel,
        out_shape=jax.ShapeDtypeStruct((n, PACK, half), BF),
        grid=(steps,),
        in_specs=[
            pl.BlockSpec((step * MAIN, both), lambda i: (i, 0)),
            pl.BlockSpec((step * 2 * REM, both), lambda i: (i, 0)),
            pl.BlockSpec(wcat.shape, lambda i: (0, 0)),
        ],
        out_specs=pl.BlockSpec((step, PACK, half), lambda i: (i, 0, 0)),
        compiler_params=pltpu.CompilerParams(vmem_limit_bytes=32 * MIB),
        cost_estimate=pl.CostEstimate(flops=2 * 1280 * width * both, bytes_accessed=10 * MIB, transcendentals=0),
        name="pair_grad",
    )(dm, dr, wcat)


def combine_kernel(ids_ref, ret_ref, out_ref, main_ref, rest_ref):
    experts, _, cols = ret_ref.shape
    toks = out_ref.shape[0]
    half = out_ref.shape[1] // 2
    c = pl.program_id(0)

    @pl.when(c == 0)
    def _():
        pos, _, _ = positions(ids_ref[...], experts)
        main, rest = select(pos)
        left = is_left(*rest.shape)
        main_ref[...] = main.T.astype(BF)
        rest_ref[0] = jnp.where(left, rest, 0.0).T.astype(BF)
        rest_ref[1] = jnp.where(left, 0.0, rest).T.astype(BF)

    tail = ret_ref[:, 2 * MAIN : PACK, :].reshape(experts * 2 * REM, cols)
    for side in range(2):
        body = ret_ref[:, side * MAIN : (side + 1) * MAIN, :].reshape(experts * MAIN, cols)
        total = dot(main_ref[...], body) + dot(rest_ref[side], tail)
        out_ref[:, pl.ds(pl.multiple_of(side * half + c * cols, 128), cols)] = total.astype(BF)


def combine(ids, ret):
    experts, _, half = ret.shape
    toks = ids.shape[0]
    steps = 4
    cols = half // steps
    return pl.pallas_call(
        combine_kernel,
        out_shape=jax.ShapeDtypeStruct((toks, 2 * half), BF),
        grid=(steps,),
        in_specs=[
            pl.BlockSpec(ids.shape, lambda c: (0, 0)),
            pl.BlockSpec((experts, PACK, cols), lambda c: (0, 0, c)),
        ],
        out_specs=pl.BlockSpec((toks, 2 * half), lambda c: (0, 0)),
        scratch_shapes=[
            pltpu.VMEM((toks, experts * MAIN), BF),
            pltpu.VMEM((2, toks, experts * 2 * REM), BF),
        ],
        compiler_params=pltpu.CompilerParams(vmem_limit_bytes=24 * MIB),
        cost_estimate=pl.CostEstimate(flops=2 * 1280 * toks * 2 * half, bytes_accessed=6 * MIB, transcendentals=0),
        name="combine",
    )(ids, ret)


def exchange(block):
    return lax.all_to_all(block, "expert", split_axis=0, concat_axis=0, tiled=True)


def shards(tokens, grad_out, gates, expert_ids, w_gate, w_up, w_down):
    experts = lax.axis_size("expert")
    copies = lax.axis_size("dp")
    wg, wu, wd = w_gate[0], w_up[0], w_down[0]
    width, hidden = wg.shape
    send_x, grad_out = lax.optimization_barrier((dispatch(expert_ids, tokens, experts), grad_out))
    rx = exchange(send_x)
    rg = exchange(dispatch(expert_ids, grad_out, experts, gates))
    csm, csr, actm, actr, wcat = forward(rx, wg, wu)
    dm, dr = hidden_grad(rg, wd, csm, csr)
    packed = weight_grad(rx, rg, dm, dr, actm, actr, copies)
    summed = lax.psum_scatter(packed, "dp", scatter_dimension=0, tiled=True)[0]
    ret = exchange(pair_grad(dm, dr, wcat))
    grad_tokens = combine(expert_ids, ret)
    grad_g, grad_u, grad_d = unpack(summed, width // copies, hidden, width, hidden // copies)
    return (grad_tokens, grad_g[None], grad_u[None], grad_d[None])


def solution(mesh):
    rows = P(("dp", "expert"), None)
    weights = P("expert", None, None)
    cut = P("expert", "dp", None)
    return jax.shard_map(
        shards,
        mesh=mesh,
        in_specs=(rows, rows, rows, rows, weights, weights, weights),
        out_specs=(rows, cut, cut, cut),
        check_vma=False,
    )
```

```python
import functools

import jax
import jax.numpy as jnp
from jax import lax
from jax.experimental import pallas as pl
from jax.experimental.pallas import tpu as pltpu
from jax.sharding import PartitionSpec as P

BF = jnp.bfloat16
F32 = jnp.float32
MIB = 1 << 20

MAIN = 32
REM = 4
PACK = 2 * (MAIN + REM)


def dot(a, b, ca=1, cb=0):
    return lax.dot_general(a, b, (((ca,), (cb,)), ((), ())), preferred_element_type=F32)


def iota(shape, dim):
    return lax.broadcasted_iota(jnp.int32, shape, dim)


def positions(ids, experts):
    toks, top = ids.shape
    ids_t = ids.astype(F32).T
    ident = iota((experts, toks), 0).astype(F32)
    member = jnp.zeros((experts, toks), F32)
    for k in range(top):
        member = member + jnp.where(ids_t[k : k + 1, :] == ident, 1.0, 0.0)
    before = (iota((toks, toks), 0) < iota((toks, toks), 1)).astype(F32).astype(BF)
    pos = dot(member.astype(BF), before)
    return jnp.where(member > 0.5, pos, -1.0), ids_t, ident


def select(pos):
    experts, toks = pos.shape
    wide = pos[:, None, :]
    main = (wide == iota((experts, MAIN, toks), 1).astype(F32)).astype(F32)
    rest = (wide == (MAIN + iota((experts, 2 * REM, toks), 1) % REM).astype(F32)).astype(F32)
    return main.reshape(experts * MAIN, toks), rest.reshape(experts * 2 * REM, toks)


def is_left(rows, cols):
    return iota((rows, cols), 0) % (2 * REM) < REM


def dispatch_kernel(scaled, *refs):
    if scaled:
        ids_ref, gates_ref, left_ref, right_ref, out_ref, main_ref, rest_ref, gmain_ref, grest_ref = refs
    else:
        ids_ref, left_ref, right_ref, out_ref, main_ref, rest_ref = refs
    experts, _, width = out_ref.shape

    @pl.when(pl.program_id(0) == 0)
    def _():
        pos, ids_t, ident = positions(ids_ref[...], experts)
        main, rest = select(pos)
        main_ref[...] = main.astype(BF)
        rest_ref[...] = rest.astype(BF)
        if scaled:
            gates_t = gates_ref[...].T
            weight = jnp.zeros(pos.shape, F32)
            for k in range(gates_t.shape[0]):
                weight = weight + jnp.where(ids_t[k : k + 1, :] == ident, gates_t[k : k + 1, :], 0.0)
            toks = pos.shape[1]
            for rows, sel, ref in ((MAIN, main, gmain_ref), (2 * REM, rest, grest_ref)):
                wide = jnp.broadcast_to(weight[:, None, :], (experts, rows, toks)).reshape(experts * rows, toks)
                ref[...] = jnp.broadcast_to(jnp.sum(sel * wide, axis=1, keepdims=True), ref.shape)

    left, right = left_ref[...], right_ref[...]

    def rows_of(sel_ref, g_ref, data):
        got = dot(sel_ref[...], data)
        if scaled:
            got = got * jnp.concatenate([g_ref[...]] * (width // 128), axis=1)
        return got

    gm = gmain_ref if scaled else None
    gr = grest_ref if scaled else None
    out_ref[:, 0:MAIN, :] = rows_of(main_ref, gm, left).astype(BF).reshape(experts, MAIN, width)
    out_ref[:, MAIN : 2 * MAIN, :] = rows_of(main_ref, gm, right).astype(BF).reshape(experts, MAIN, width)
    rest_l = rows_of(rest_ref, gr, left)
    rest_r = rows_of(rest_ref, gr, right)
    both = jnp.where(is_left(*rest_l.shape), rest_l, rest_r)
    out_ref[:, 2 * MAIN : PACK, :] = both.astype(BF).reshape(experts, 2 * REM, width)


def dispatch(ids, data, experts, gates=None):
    toks, width = data.shape
    half, steps = width // 2, 4
    cols = half // steps
    full = lambda a: pl.BlockSpec(a.shape, lambda c: (0,) * a.ndim)
    small = [ids] if gates is None else [ids, gates]
    scratch = [pltpu.VMEM((experts * MAIN, toks), BF), pltpu.VMEM((experts * 2 * REM, toks), BF)]
    if gates is not None:
        scratch += [pltpu.VMEM((experts * MAIN, 128), F32), pltpu.VMEM((experts * 2 * REM, 128), F32)]
    return pl.pallas_call(
        functools.partial(dispatch_kernel, gates is not None),
        out_shape=pltpu.HBM((experts, PACK, half), BF),
        grid=(steps,),
        in_specs=[full(a) for a in small]
        + [pl.BlockSpec((toks, cols), lambda c: (0, c)), pl.BlockSpec((toks, cols), lambda c: (0, c + steps))],
        out_specs=pl.BlockSpec((experts, PACK, cols), lambda c: (0, 0, c)),
        scratch_shapes=scratch,
        compiler_params=pltpu.CompilerParams(vmem_limit_bytes=28 * MIB),
        cost_estimate=pl.CostEstimate(flops=2 * 1280 * toks * width, bytes_accessed=6 * MIB, transcendentals=0),
        name="dispatch",
    )(*small, data, data)


def halves(ref):
    n, _, half = ref.shape
    rest = ref[:, 2 * MAIN : PACK, :].reshape(n * 2 * REM, half)
    left = ref[:, 0:MAIN, :].reshape(n * MAIN, half)
    right = ref[:, MAIN : 2 * MAIN, :].reshape(n * MAIN, half)
    return jnp.concatenate([left, rest], axis=0), jnp.concatenate([right, rest], axis=0)


def joined(p_left, p_right, mains):
    main = p_left[:mains] + p_right[:mains]
    tail = p_right[mains:]
    rest = p_left[mains:] + pltpu.roll(tail, tail.shape[0] - REM, 0)
    return main, jnp.where(is_left(*rest.shape), rest, 0.0)


def forward_kernel(x_ref, wg_ref, wu_ref, csm_ref, csr_ref, actm_ref, actr_ref, wcat_ref):
    hidden = wg_ref.shape[1]
    half = x_ref.shape[2]

    @pl.when(pl.program_id(0) == 0)
    def _():
        wcat_ref[:, :hidden] = wg_ref[...]
        wcat_ref[:, hidden:] = wu_ref[...]

    mains = x_ref.shape[0] * MAIN
    a_left, a_right = halves(x_ref)
    pre = joined(dot(a_left, wcat_ref[:half, :]), dot(a_right, wcat_ref[half:, :]), mains)
    for p, cs_ref, act_ref in zip(pre, (csm_ref, csr_ref), (actm_ref, actr_ref)):
        gate, up = p[:, :hidden], p[:, hidden:]
        sigma = jax.nn.sigmoid(gate)
        silu = gate * sigma
        cs_ref[:, :hidden] = up * sigma * (1.0 + gate * (1.0 - sigma))
        cs_ref[:, hidden:] = silu
        act_ref[...] = (silu * up).astype(BF)


def forward(rx, wg, wu):
    n, _, half = rx.shape
    width, hidden = wg.shape
    steps = 4
    step = n // steps
    rows = lambda per, cols: pl.BlockSpec((step * per, cols), lambda i: (i, 0))
    full = lambda shape: pl.BlockSpec(shape, lambda i: (0, 0))
    mains, rests = n * MAIN, n * 2 * REM
    return pl.pallas_call(
        forward_kernel,
        out_shape=(
            jax.ShapeDtypeStruct((mains, 2 * hidden), F32),
            jax.ShapeDtypeStruct((rests, 2 * hidden), F32),
            jax.ShapeDtypeStruct((mains, hidden), BF),
            jax.ShapeDtypeStruct((rests, hidden), BF),
            jax.ShapeDtypeStruct((width, 2 * hidden), BF),
        ),
        grid=(steps,),
        in_specs=[
            pl.BlockSpec((step, PACK, half), lambda i: (i, 0, 0)),
            full((width, hidden)),
            full((width, hidden)),
        ],
        out_specs=(
            rows(MAIN, 2 * hidden),
            rows(2 * REM, 2 * hidden),
            rows(MAIN, hidden),
            rows(2 * REM, hidden),
            full((width, 2 * hidden)),
        ),
        compiler_params=pltpu.CompilerParams(vmem_limit_bytes=28 * MIB),
        cost_estimate=pl.CostEstimate(
            flops=2 * (mains + rests) * width * 2 * hidden, bytes_accessed=16 * MIB, transcendentals=mains * hidden
        ),
        name="forward",
    )(rx, wg, wu)


def shifted(rest):
    return pltpu.roll(rest.astype(F32), REM, 0)


def middle_kernel(
    g_ref, x_ref, wd_ref, wcat_ref, csm_ref, csr_ref, actm_ref, actr_ref,
    packed_hbm, pair_ref,
    dm_ref, dr_ref, dt_ref, at_ref, packed_ref, sem,
):
    copies = packed_ref.shape[0]
    n, _, half = x_ref.shape
    mains = n * MAIN
    both, hidden = dm_ref.shape[1], wd_ref.shape[0]
    parts = 4
    step = n // parts
    most, few = step * MAIN, step * 2 * REM

    main = actm_ref[...].T
    at_ref[0, :, :mains] = main
    at_ref[1, :, :mains] = main
    rest = actr_ref[...]
    at_ref[0, :, mains:] = rest.T
    at_ref[1, :, mains:] = shifted(rest).astype(BF).T

    for i in range(parts):
        a_left, a_right = halves(g_ref.at[i * step : (i + 1) * step])
        d_act = joined(dot(a_left, wd_ref[:, :half], 1, 1), dot(a_right, wd_ref[:, half:], 1, 1), most)
        for d, cs_ref, d_ref, per, base in zip(
            d_act, (csm_ref, csr_ref), (dm_ref, dr_ref), (most, few), (0, mains)
        ):
            rows = slice(i * per, (i + 1) * per)
            cols = slice(base + i * per, base + (i + 1) * per)
            grad = jnp.concatenate([d, d], axis=1) * cs_ref[rows, :]
            low = grad.astype(BF)
            d_ref[rows, :] = low
            turned = low.T
            dt_ref[0, :, cols] = turned
            dt_ref[1, :, cols] = turned if base == 0 else pltpu.roll(grad, REM, 0).astype(BF).T

    tile = 256
    per = 2 * half // copies
    slab = hidden // copies
    base = both * per // 128
    for side in range(2):
        for j in range(half // tile):
            cols = slice(j * tile, (j + 1) * tile)

            def rows_of(ref):
                body = ref[:, side * MAIN : (side + 1) * MAIN, cols].reshape(mains, tile)
                tail = ref[:, 2 * MAIN : PACK, cols].reshape(n * 2 * REM, tile)
                return jnp.concatenate([body, tail], axis=0)

            into = dot(dt_ref[side], rows_of(x_ref)).astype(BF)
            down = dot(at_ref[side], rows_of(g_ref)).astype(BF)
            for q in range(tile // 128):
                at = (side * half + j * tile) // 128 + q
                owner, piece = at * 128 // per, at % (per // 128)
                part = into[:, q * 128 : (q + 1) * 128]
                packed_ref[owner, piece * both : (piece + 1) * both, :] = part
                part = down[:, q * 128 : (q + 1) * 128].reshape(copies, slab, 128)
                packed_ref[:, base + at * slab : base + (at + 1) * slab, :] = part
    packed_out = pltpu.make_async_copy(packed_ref, packed_hbm, sem)
    packed_out.start()

    for i in range(parts):
        main = dm_ref[i * most : (i + 1) * most, :]
        rest = dr_ref[i * few : (i + 1) * few, :]
        d_left = jnp.concatenate([main, rest], axis=0)
        d_right = jnp.concatenate([main, shifted(rest).astype(BF)], axis=0)
        y_left = dot(d_left, wcat_ref[:half, :], 1, 1)
        y_right = dot(d_right, wcat_ref[half:, :], 1, 1)
        some = slice(i * step, (i + 1) * step)
        pair_ref[some, 0:MAIN, :] = y_left[:most].astype(BF).reshape(step, MAIN, half)
        pair_ref[some, MAIN : 2 * MAIN, :] = y_right[:most].astype(BF).reshape(step, MAIN, half)
        tail = (y_left[most:] + y_right[most:]).astype(BF)
        pair_ref[some, 2 * MAIN : PACK, :] = tail.reshape(step, 2 * REM, half)
    packed_out.wait()


def middle(rg, rx, wd, wcat, csm, csr, actm, actr, copies):
    n, _, half = rx.shape
    both, hidden = csm.shape[1], wd.shape[0]
    mains, rests = csm.shape[0], csr.shape[0]
    rows = mains + rests
    length = 3 * hidden * 2 * half // copies // 128
    vmem = pl.BlockSpec(memory_space=pltpu.VMEM)
    hbm = pl.BlockSpec(memory_space=pltpu.HBM)
    return pl.pallas_call(
        middle_kernel,
        out_shape=(pltpu.HBM((copies, length, 128), BF), jax.ShapeDtypeStruct((n, PACK, half), BF)),
        in_specs=[vmem] * 8,
        out_specs=(hbm, vmem),
        scratch_shapes=[
            pltpu.VMEM((mains, both), BF),
            pltpu.VMEM((rests, both), BF),
            pltpu.VMEM((2, both, rows), BF),
            pltpu.VMEM((2, hidden, rows), BF),
            pltpu.VMEM((copies, length, 128), BF),
            pltpu.SemaphoreType.DMA,
        ],
        compiler_params=pltpu.CompilerParams(vmem_limit_bytes=32 * MIB),
        cost_estimate=pl.CostEstimate(
            flops=2 * rows * 2 * half * 6 * hidden, bytes_accessed=28 * MIB, transcendentals=0
        ),
        name="middle",
    )(rg, rx, wd, wcat, csm, csr, actm, actr)


def unpack_kernel(in_ref, gate_ref, up_ref, down_ref):
    per, hidden = gate_ref.shape
    slab = down_ref.shape[0]
    base = 2 * hidden * per // 128
    for q in range(per // 128):
        both = in_ref[q * 2 * hidden : (q + 1) * 2 * hidden, :].T
        gate_ref[q * 128 : (q + 1) * 128, :] = both[:, :hidden]
        up_ref[q * 128 : (q + 1) * 128, :] = both[:, hidden:]
    for q in range(down_ref.shape[1] // 128):
        down_ref[:, q * 128 : (q + 1) * 128] = in_ref[base + q * slab : base + (q + 1) * slab, :]


def unpack(summed, per, hidden, width, slab):
    vmem = pl.BlockSpec(memory_space=pltpu.VMEM)
    return pl.pallas_call(
        unpack_kernel,
        out_shape=(
            jax.ShapeDtypeStruct((per, hidden), BF),
            jax.ShapeDtypeStruct((per, hidden), BF),
            jax.ShapeDtypeStruct((slab, width), BF),
        ),
        in_specs=[vmem],
        out_specs=(vmem, vmem, vmem),
        cost_estimate=pl.CostEstimate(flops=0, bytes_accessed=2 * MIB, transcendentals=0),
        name="unpack",
    )(summed)


def combine_kernel(ids_ref, ret_ref, out_ref, main_ref, rest_ref):
    experts, _, cols = ret_ref.shape
    toks = out_ref.shape[0]
    half = out_ref.shape[1] // 2
    c = pl.program_id(0)

    @pl.when(c == 0)
    def _():
        pos, _, _ = positions(ids_ref[...], experts)
        main, rest = select(pos)
        left = is_left(*rest.shape)
        main_ref[...] = main.T.astype(BF)
        rest_ref[0] = jnp.where(left, rest, 0.0).T.astype(BF)
        rest_ref[1] = jnp.where(left, 0.0, rest).T.astype(BF)

    tail = ret_ref[:, 2 * MAIN : PACK, :].reshape(experts * 2 * REM, cols)
    for side in range(2):
        body = ret_ref[:, side * MAIN : (side + 1) * MAIN, :].reshape(experts * MAIN, cols)
        total = dot(main_ref[...], body) + dot(rest_ref[side], tail)
        out_ref[:, pl.ds(pl.multiple_of(side * half + c * cols, 128), cols)] = total.astype(BF)


def combine(ids, ret):
    experts, _, half = ret.shape
    toks = ids.shape[0]
    steps = 4
    cols = half // steps
    return pl.pallas_call(
        combine_kernel,
        out_shape=jax.ShapeDtypeStruct((toks, 2 * half), BF),
        grid=(steps,),
        in_specs=[
            pl.BlockSpec(ids.shape, lambda c: (0, 0)),
            pl.BlockSpec((experts, PACK, cols), lambda c: (0, 0, c)),
        ],
        out_specs=pl.BlockSpec((toks, 2 * half), lambda c: (0, 0)),
        scratch_shapes=[
            pltpu.VMEM((toks, experts * MAIN), BF),
            pltpu.VMEM((2, toks, experts * 2 * REM), BF),
        ],
        compiler_params=pltpu.CompilerParams(vmem_limit_bytes=24 * MIB),
        cost_estimate=pl.CostEstimate(flops=2 * 1280 * toks * 2 * half, bytes_accessed=6 * MIB, transcendentals=0),
        name="combine",
    )(ids, ret)


def exchange(block):
    return lax.all_to_all(block, "expert", split_axis=0, concat_axis=0, tiled=True)


def shards(tokens, grad_out, gates, expert_ids, w_gate, w_up, w_down):
    experts = lax.axis_size("expert")
    copies = lax.axis_size("dp")
    wg, wu, wd = w_gate[0], w_up[0], w_down[0]
    width, hidden = wg.shape
    send_x, grad_out = lax.optimization_barrier((dispatch(expert_ids, tokens, experts), grad_out))
    rx = exchange(send_x)
    rg = exchange(dispatch(expert_ids, grad_out, experts, gates))
    csm, csr, actm, actr, wcat = forward(rx, wg, wu)
    packed, outgoing = middle(rg, rx, wd, wcat, csm, csr, actm, actr, copies)
    summed = lax.psum_scatter(packed, "dp", scatter_dimension=0, tiled=True)[0]
    ret = exchange(outgoing)
    grad_tokens = combine(expert_ids, ret)
    grad_g, grad_u, grad_d = unpack(summed, width // copies, hidden, width, hidden // copies)
    return (grad_tokens, grad_g[None], grad_u[None], grad_d[None])


def solution(mesh):
    rows = P(("dp", "expert"), None)
    weights = P("expert", None, None)
    cut = P("expert", "dp", None)
    return jax.shard_map(
        shards,
        mesh=mesh,
        in_specs=(rows, rows, rows, rows, weights, weights, weights),
        out_specs=(rows, cut, cut, cut),
        check_vma=False,
    )
```

```python
import functools

import jax
import jax.numpy as jnp
from jax import lax
from jax.experimental import pallas as pl
from jax.experimental.pallas import tpu as pltpu
from jax.sharding import PartitionSpec as P

BF = jnp.bfloat16
F32 = jnp.float32
MIB = 1 << 20

MAIN = 32
REM = 4
PACK = 2 * (MAIN + REM)


def dot(a, b, ca=1, cb=0):
    return lax.dot_general(a, b, (((ca,), (cb,)), ((), ())), preferred_element_type=F32)


def iota(shape, dim):
    return lax.broadcasted_iota(jnp.int32, shape, dim)


def positions(ids, experts):
    top, toks = ids.shape
    ids_t = ids.astype(F32)
    ident = iota((experts, toks), 0).astype(F32)
    member = jnp.zeros((experts, toks), F32)
    for k in range(top):
        member = member + jnp.where(ids_t[k : k + 1, :] == ident, 1.0, 0.0)
    before = (iota((toks, toks), 0) < iota((toks, toks), 1)).astype(F32).astype(BF)
    pos = dot(member.astype(BF), before)
    return jnp.where(member > 0.5, pos, -1.0), ids_t, ident


def select(pos):
    experts, toks = pos.shape
    wide = pos[:, None, :]
    main = (wide == iota((experts, MAIN, toks), 1).astype(F32)).astype(F32)
    rest = (wide == (MAIN + iota((experts, 2 * REM, toks), 1) % REM).astype(F32)).astype(F32)
    return main.reshape(experts * MAIN, toks), rest.reshape(experts * 2 * REM, toks)


def is_left(rows, cols):
    return iota((rows, cols), 0) % (2 * REM) < REM


def prepare_kernel(ids_ref, gates_ref, tokens_hbm, grads_hbm, tokens_out, grads_out, extra_ref, sems):
    width = tokens_hbm.shape[1]
    copies = [
        pltpu.make_async_copy(tokens_hbm, tokens_out.at[:, :width], sems.at[0]),
        pltpu.make_async_copy(grads_hbm, grads_out.at[:, :width], sems.at[1]),
    ]
    for copy in copies:
        copy.start()
    pos, ids_t, ident = positions(ids_ref[...], 32)
    gates_t = gates_ref[...]
    weight = jnp.zeros(pos.shape, F32)
    for k in range(gates_t.shape[0]):
        weight = weight + jnp.where(ids_t[k : k + 1, :] == ident, gates_t[k : k + 1, :], 0.0)
    high = weight.astype(BF).astype(F32)
    mid = (weight - high).astype(BF).astype(F32)
    low = weight - high - mid
    extra_ref[...] = jnp.concatenate([pos, high, mid, low], axis=0).T.astype(BF)
    for n, dst in enumerate((tokens_out, grads_out)):
        copies.append(pltpu.make_async_copy(extra_ref, dst.at[:, width:], sems.at[2 + n]))
        copies[-1].start()
    for copy in copies:
        copy.wait()


HBM = pl.BlockSpec(memory_space=pltpu.HBM)
VMEM = pl.BlockSpec(memory_space=pltpu.VMEM)


def prepare(ids, gates, tokens, grads):
    toks, width = tokens.shape
    shape = pltpu.HBM((toks, width + 128), BF)
    return pl.pallas_call(
        prepare_kernel,
        out_shape=(shape, shape),
        in_specs=[VMEM, VMEM, HBM, HBM],
        out_specs=(HBM, HBM),
        scratch_shapes=[pltpu.VMEM((toks, 128), BF), pltpu.SemaphoreType.DMA((4,))],
        compiler_params=pltpu.CompilerParams(vmem_limit_bytes=16 * MIB),
        cost_estimate=pl.CostEstimate(flops=1 << 20, bytes_accessed=2 * MIB, transcendentals=0),
        name="prepare",
    )(ids, gates, tokens, grads)


def dispatch_kernel(scaled, per, wanted_ref, slot_ref, *refs):
    lines = 4
    sources = refs[:lines]
    count = 8 if scaled else 1
    outs = refs[lines : lines + count]
    data_ref, s_ref, out_ref, scale_ref, in_sems, out_sems = refs[lines + count :]
    experts, rows, width = out_ref.shape
    toks = sources[0].shape[0]

    loads = [
        pltpu.make_async_copy(src, data_ref.at[k * toks : (k + 1) * toks, :], in_sems.at[k])
        for k, src in enumerate(sources)
    ]
    for load in loads:
        load.start()
    for load in loads:
        load.wait()

    extra = data_ref[:, width:]
    wanted = wanted_ref[...]
    lane = iota(wanted.shape, 1)

    def column(piece):
        pick = (lane == wanted + piece * 32).astype(F32).astype(BF)
        return dot(pick, extra, 1, 1)

    pos = column(0)
    target = jnp.where(pos >= 0.0, pos + slot_ref[0:1, :].astype(F32) * float(per), -1.0)
    chosen = target[:, None, :] == iota((experts, rows, lines * toks), 1).astype(F32)
    chosen = chosen.astype(F32)
    s_ref[...] = chosen.reshape(experts * rows, lines * toks).astype(BF)
    if scaled:
        weight = column(1) + (column(2) + column(3))
        total = jnp.sum(chosen * weight[:, None, :], axis=2, keepdims=True)
        scale_ref[...] = jnp.broadcast_to(total, (experts, rows, 128)).reshape(experts * rows, 128)

    stores = []
    parts = 4
    columns = width // parts
    for c in range(parts):
        cols = slice(c * columns, (c + 1) * columns)
        got = dot(s_ref[...], data_ref[:, cols])
        if scaled:
            got = got * jnp.concatenate([scale_ref[...]] * (columns // 128), axis=1)
        out_ref[:, :, cols] = got.astype(BF).reshape(experts, rows, columns)
        for k, out in enumerate(outs):
            here, there = (out_ref.at[k], out) if scaled else (out_ref, out)
            at = (slice(None),) * (len(there.shape) - 1) + (cols,)
            stores.append(pltpu.make_async_copy(here.at[at], there.at[at], out_sems.at[c * count + k]))
            stores[-1].start()
    for store in stores:
        store.wait()


def dispatch(wanted, slots, lines, scaled):
    toks, width = lines[0].shape[0], lines[0].shape[1] - 128
    per, experts = MAIN + REM, 8
    rows, all_toks = len(lines) * per, len(lines) * toks
    shapes = (pltpu.HBM((rows, width), BF),) * experts if scaled else (pltpu.HBM((experts, rows, width), BF),)
    return pl.pallas_call(
        functools.partial(dispatch_kernel, scaled, per),
        out_shape=shapes,
        in_specs=[VMEM, VMEM] + [HBM] * len(lines),
        out_specs=(HBM,) * len(shapes),
        scratch_shapes=[
            pltpu.VMEM((all_toks, width + 128), BF),
            pltpu.VMEM((experts * rows, all_toks), BF),
            pltpu.VMEM((experts, rows, width), BF),
            pltpu.VMEM((experts * rows, 128), F32),
            pltpu.SemaphoreType.DMA((len(lines),)),
            pltpu.SemaphoreType.DMA((4 * len(shapes),)),
        ],
        compiler_params=pltpu.CompilerParams(vmem_limit_bytes=32 * MIB),
        cost_estimate=pl.CostEstimate(
            flops=2 * experts * rows * all_toks * width, bytes_accessed=7 * MIB, transcendentals=0
        ),
        name="dispatch",
    )(wanted, slots, *lines)


def regrouped(block):
    return block % 4 * 8 + block // 4 % 2 * 4 + block // 8


def forward_kernel(*refs):
    blocks, wg_hbm, wu_hbm = refs[:3]
    cs_hbm, act_hbm, wcat_hbm = refs[3:6]
    x_ref, wcat_ref, cs_ref, act_ref, turn_ref, at_ref, sems = refs[6:]
    rows = blocks.shape[1]
    hidden = wg_hbm.shape[1]
    loads = [
        pltpu.make_async_copy(wg_hbm, wcat_ref.at[:, :hidden], sems.at[8]),
        pltpu.make_async_copy(wu_hbm, wcat_ref.at[:, hidden:], sems.at[9]),
    ]
    loads += [
        pltpu.make_async_copy(blocks.at[k], x_ref.at[k * rows : (k + 1) * rows, :], sems.at[k]) for k in range(8)
    ]
    for load in loads:
        load.start()
    loads[0].wait()
    loads[1].wait()
    stores = [pltpu.make_async_copy(wcat_ref, wcat_hbm, sems.at[10])]
    stores[0].start()
    parts = 2
    most = 8 // parts * rows
    for i in range(parts):
        for load in loads[2 + i * 8 // parts : 2 + (i + 1) * 8 // parts]:
            load.wait()
        some = slice(i * most, (i + 1) * most)
        pre = dot(x_ref[some, :], wcat_ref[...])
        gate, up = pre[:, :hidden], pre[:, hidden:]
        sigma = jax.nn.sigmoid(gate)
        silu = gate * sigma
        cs_ref[some, :hidden] = up * sigma * (1.0 + gate * (1.0 - sigma))
        cs_ref[some, hidden:] = silu
        act_ref[some, :] = silu * up
        store = pltpu.make_async_copy(cs_ref.at[some, :], cs_hbm.at[some, :], sems.at[11 + i])
        store.start()
        stores.append(store)
    per = MAIN + REM
    for b in range(32):
        to = regrouped(b)
        turn_ref[to * per : (to + 1) * per, :] = act_ref[b * per : (b + 1) * per, :]
    at_ref[...] = turn_ref[...].astype(BF).T
    stores.append(pltpu.make_async_copy(at_ref, act_hbm, sems.at[13]))
    stores[-1].start()
    for store in stores:
        store.wait()


def forward(blocks, wg, wu):
    width, hidden = wg.shape
    rows = 8 * blocks.shape[1]
    return pl.pallas_call(
        forward_kernel,
        out_shape=(
            pltpu.HBM((rows, 2 * hidden), F32),
            pltpu.HBM((hidden, rows), BF),
            pltpu.HBM((width, 2 * hidden), BF),
        ),
        in_specs=[HBM] * 3,
        out_specs=(HBM,) * 3,
        scratch_shapes=[
            pltpu.VMEM((rows, width), BF),
            pltpu.VMEM((width, 2 * hidden), BF),
            pltpu.VMEM((rows, 2 * hidden), F32),
            pltpu.VMEM((rows, hidden), F32),
            pltpu.VMEM((rows, hidden), F32),
            pltpu.VMEM((hidden, rows), BF),
            pltpu.SemaphoreType.DMA((14,)),
        ],
        compiler_params=pltpu.CompilerParams(vmem_limit_bytes=36 * MIB),
        cost_estimate=pl.CostEstimate(
            flops=2 * rows * width * 2 * hidden, bytes_accessed=16 * MIB, transcendentals=rows * hidden
        ),
        name="forward",
    )(blocks, wg, wu)


def middle_kernel(*refs):
    to_ref, at_row_ref, gs, xs = refs[0], refs[1], refs[2:10], refs[10]
    wd_hbm, wcat_hbm, cs_hbm, act_hbm = refs[11:15]
    packed_hbm, pair_hbm = refs[15:17]
    (g_ref, x_ref, wd_ref, wcat_ref, cs_ref, at_ref, raw_ref, turn_ref, d_ref, dt_ref, dm_ref, dr_ref, packed_ref,
     pair_ref, sems, out_sems) = refs[17:]
    rows = gs[0].shape[0]
    copies = packed_ref.shape[0]
    n, _, half = pair_ref.shape
    hidden, both = at_ref.shape[0], wcat_ref.shape[1]
    per_block = MAIN + REM

    def load(src, dst, sem):
        copy = pltpu.make_async_copy(src, dst, sems.at[sem])
        copy.start()
        return copy

    wd_in = load(wd_hbm, wd_ref, 16)
    g_in = [
        load(b, g_ref.at[pl.ds(pl.multiple_of(at_row_ref[k], 16), rows), :], k) for k, b in enumerate(gs)
    ]
    cs_in = load(cs_hbm, cs_ref, 17)
    x_in = [load(xs.at[k], x_ref.at[k * rows : (k + 1) * rows, :], 8 + k) for k in range(8)]
    act_in = load(act_hbm, at_ref, 18)
    wcat_in = load(wcat_hbm, wcat_ref, 19)

    wd_in.wait()
    parts = 4
    most = 8 // parts * rows
    for i in range(parts):
        for copy in g_in[i * 8 // parts : (i + 1) * 8 // parts]:
            copy.wait()
        some = slice(i * most, (i + 1) * most)
        raw_ref[some, :] = dot(g_ref[some, :], wd_ref[...], 1, 1)
    for b in range(n):
        to = regrouped(b)
        turn_ref[to * per_block : (to + 1) * per_block, :] = raw_ref[b * per_block : (b + 1) * per_block, :]
    cs_in.wait()
    for i in range(parts):
        some = slice(i * most, (i + 1) * most)
        d_act = turn_ref[some, :]
        grad = jnp.concatenate([d_act, d_act], axis=1) * cs_ref[some, :]
        d_ref[some, :] = grad
    dt_ref[...] = d_ref[...].astype(BF).T
    dr_ref[...] = jnp.zeros_like(dr_ref)
    for b in range(n):
        dm_ref[b * MAIN : (b + 1) * MAIN, :] = d_ref[b * per_block : b * per_block + MAIN, :].astype(BF)
        dr_ref[b * 2 * REM : b * 2 * REM + REM, :] = d_ref[b * per_block + MAIN : (b + 1) * per_block, :]

    for copy in x_in:
        copy.wait()
    act_in.wait()
    tile = 256
    per = 2 * half // copies
    slab = hidden // copies
    base = both * per // 128
    for j in range(2 * half // tile):
        cols = slice(j * tile, (j + 1) * tile)
        into = dot(dt_ref[...], x_ref[:, cols]).astype(BF)
        down = dot(at_ref[...], g_ref[:, cols]).astype(BF)
        for q in range(tile // 128):
            at = j * tile // 128 + q
            owner, piece = at * 128 // per, at % (per // 128)
            part = into[:, q * 128 : (q + 1) * 128]
            packed_ref[owner, piece * both : (piece + 1) * both, :] = part
            part = down[:, q * 128 : (q + 1) * 128].reshape(copies, slab, 128)
            packed_ref[:, base + at * slab : base + (at + 1) * slab, :] = part
    packed_out = pltpu.make_async_copy(packed_ref, packed_hbm, out_sems.at[n])
    packed_out.start()

    wcat_in.wait()
    sent = []
    step = n // parts
    most, few = step * MAIN, step * 2 * REM
    for i in range(parts):
        main = dm_ref[i * most : (i + 1) * most, :]
        rest = dr_ref[i * few : (i + 1) * few, :]
        d_left = jnp.concatenate([main, rest.astype(BF)], axis=0)
        d_right = jnp.concatenate([main, pltpu.roll(rest, REM, 0).astype(BF)], axis=0)
        y_left = dot(d_left, wcat_ref[:half, :], 1, 1)
        y_right = dot(d_right, wcat_ref[half:, :], 1, 1)
        some = slice(i * step, (i + 1) * step)
        pair_ref[some, 0:MAIN, :] = y_left[:most].astype(BF).reshape(step, MAIN, half)
        pair_ref[some, MAIN : 2 * MAIN, :] = y_right[:most].astype(BF).reshape(step, MAIN, half)
        tail = (y_left[most:] + y_right[most:]).astype(BF)
        pair_ref[some, 2 * MAIN : PACK, :] = tail.reshape(step, 2 * REM, half)
        for b in range(i * step, (i + 1) * step):
            copy = pltpu.make_async_copy(pair_ref.at[b], pair_hbm.at[to_ref[b]], out_sems.at[b])
            copy.start()
            sent.append(copy)
    for copy in sent:
        copy.wait()
    packed_out.wait()


def middle(to, at_row, gs, xs, wd, wcat, cs, act, copies):
    hidden, width = wd.shape
    both, rows = cs.shape[1], cs.shape[0]
    n, half = to.shape[0], width // 2
    length = 3 * hidden * width // copies // 128
    smem = pl.BlockSpec(memory_space=pltpu.SMEM)
    return pl.pallas_call(
        middle_kernel,
        out_shape=(pltpu.HBM((copies, length, 128), BF), pltpu.HBM((n, PACK, half), BF)),
        in_specs=[smem] * 2 + [HBM] * 13,
        out_specs=(HBM,) * 2,
        scratch_shapes=[
            pltpu.VMEM((rows, width), BF),
            pltpu.VMEM((rows, width), BF),
            pltpu.VMEM((hidden, width), BF),
            pltpu.VMEM((width, both), BF),
            pltpu.VMEM((rows, both), F32),
            pltpu.VMEM((hidden, rows), BF),
            pltpu.VMEM((rows, hidden), F32),
            pltpu.VMEM((rows, hidden), F32),
            pltpu.VMEM((rows, both), F32),
            pltpu.VMEM((both, rows), BF),
            pltpu.VMEM((n * MAIN, both), BF),
            pltpu.VMEM((n * 2 * REM, both), F32),
            pltpu.VMEM((copies, length, 128), BF),
            pltpu.VMEM((n, PACK, half), BF),
            pltpu.SemaphoreType.DMA((20,)),
            pltpu.SemaphoreType.DMA((n + 1,)),
        ],
        compiler_params=pltpu.CompilerParams(vmem_limit_bytes=50 * MIB),
        cost_estimate=pl.CostEstimate(flops=2 * rows * width * 6 * hidden, bytes_accessed=28 * MIB, transcendentals=0),
        name="middle",
    )(to, at_row, *gs, xs, wd, wcat, cs, act)


def unpack_kernel(in_ref, gate_ref, up_ref, down_ref):
    per, hidden = gate_ref.shape
    slab = down_ref.shape[0]
    base = 2 * hidden * per // 128
    for q in range(per // 128):
        both = in_ref[q * 2 * hidden : (q + 1) * 2 * hidden, :].T
        gate_ref[q * 128 : (q + 1) * 128, :] = both[:, :hidden]
        up_ref[q * 128 : (q + 1) * 128, :] = both[:, hidden:]
    for q in range(down_ref.shape[1] // 128):
        down_ref[:, q * 128 : (q + 1) * 128] = in_ref[base + q * slab : base + (q + 1) * slab, :]


def unpack(summed, per, hidden, width, slab):
    vmem = pl.BlockSpec(memory_space=pltpu.VMEM)
    return pl.pallas_call(
        unpack_kernel,
        out_shape=(
            jax.ShapeDtypeStruct((per, hidden), BF),
            jax.ShapeDtypeStruct((per, hidden), BF),
            jax.ShapeDtypeStruct((slab, width), BF),
        ),
        in_specs=[vmem],
        out_specs=(vmem, vmem, vmem),
        cost_estimate=pl.CostEstimate(flops=0, bytes_accessed=2 * MIB, transcendentals=0),
        name="unpack",
    )(summed)


def combine_kernel(ids_ref, ret_ref, out_ref, main_ref, rest_ref):
    experts, _, cols = ret_ref.shape
    toks = out_ref.shape[0]
    half = out_ref.shape[1] // 2
    c = pl.program_id(0)

    @pl.when(c == 0)
    def _():
        pos, _, _ = positions(ids_ref[...], experts)
        main, rest = select(pos)
        left = is_left(*rest.shape)
        main_ref[...] = main.T.astype(BF)
        rest_ref[0] = jnp.where(left, rest, 0.0).T.astype(BF)
        rest_ref[1] = jnp.where(left, 0.0, rest).T.astype(BF)

    tail = ret_ref[:, 2 * MAIN : PACK, :].reshape(experts * 2 * REM, cols)
    for side in range(2):
        body = ret_ref[:, side * MAIN : (side + 1) * MAIN, :].reshape(experts * MAIN, cols)
        total = dot(main_ref[...], body) + dot(rest_ref[side], tail)
        out_ref[:, pl.ds(pl.multiple_of(side * half + c * cols, 128), cols)] = total.astype(BF)


def combine(ids, ret):
    experts, _, half = ret.shape
    toks = ids.shape[1]
    steps = 4
    cols = half // steps
    return pl.pallas_call(
        combine_kernel,
        out_shape=jax.ShapeDtypeStruct((toks, 2 * half), BF),
        grid=(steps,),
        in_specs=[
            pl.BlockSpec(ids.shape, lambda c: (0, 0)),
            pl.BlockSpec((experts, PACK, cols), lambda c: (0, 0, c)),
        ],
        out_specs=pl.BlockSpec((toks, 2 * half), lambda c: (0, 0)),
        scratch_shapes=[
            pltpu.VMEM((toks, experts * MAIN), BF),
            pltpu.VMEM((2, toks, experts * 2 * REM), BF),
        ],
        compiler_params=pltpu.CompilerParams(vmem_limit_bytes=24 * MIB),
        cost_estimate=pl.CostEstimate(flops=2 * 1280 * toks * 2 * half, bytes_accessed=6 * MIB, transcendentals=0),
        name="combine",
    )(ids, ret)


SIDE = 4
CORES = 2
SHIFTS = [(d, f) for d in range(SIDE) for f in range(CORES)]


def place(x, y, core):
    return (x % SIDE * SIDE + y % SIDE) * CORES + core


def moved(value, dx, dy, flip):
    if dx == dy == flip == 0:
        return value
    pairs = []
    for x in range(SIDE):
        for y in range(SIDE):
            for core in range(CORES):
                pairs.append((place(x, y, core), place(x + dx, y + dy, core ^ flip)))
    return lax.ppermute(value, "expert", pairs)


def shards(tokens, grad_out, gates, expert_ids, w_gate, w_up, w_down):
    copies = lax.axis_size("dp")
    wg, wu, wd = w_gate[0], w_up[0], w_down[0]
    width, hidden = wg.shape
    me = lax.axis_index("expert")
    x, y, core = me // (SIDE * CORES), me // CORES % SIDE, me % CORES
    wide = lambda values: jnp.broadcast_to(jnp.stack(values).astype(jnp.int32)[:, None], (len(values), 128))
    along_y = wide([place(x, d, f) for d, f in SHIFTS])
    along_x = wide([place(x + d, y, core ^ f) for d, f in SHIFTS])
    toks = tokens.shape[0]
    near = jnp.arange(SIDE, dtype=jnp.int32)
    slots_x = jnp.broadcast_to(jnp.repeat(near, toks)[None, :], (8, SIDE * toks))
    slots_g = jnp.broadcast_to(jnp.repeat((y - near + SIDE) % SIDE, toks)[None, :], (8, SIDE * toks))
    origin = jnp.stack([place(x - d + SIDE, b, f) for b, f in SHIFTS for d in range(SIDE)]).astype(jnp.int32)
    at_row = jnp.stack([(d * CORES + (core ^ f)) * SIDE * (MAIN + REM) for d, f in SHIFTS]).astype(jnp.int32)

    ids_t = expert_ids.T
    tokens, grad_out = prepare(ids_t, gates.T, tokens, grad_out)
    lines_x = [moved(tokens, d, 0, 0) for d in range(SIDE)]
    lines_g = [moved(grad_out, 0, d, 0) for d in range(SIDE)]
    lines_x, lines_g = lax.optimization_barrier((lines_x, lines_g))
    (out_x,) = dispatch(along_y, slots_x, lines_x, False)
    columns = [[place(a, b, f) for b in range(SIDE) for f in range(CORES)] for a in range(SIDE)]
    xs = lax.all_to_all(out_x, "expert", split_axis=0, concat_axis=0, axis_index_groups=columns, tiled=True)
    along_x, _ = lax.optimization_barrier((along_x, out_x))
    out_g = dispatch(along_x, slots_g, lines_g, True)
    gs = [moved(v, d, 0, f) for v, (d, f) in zip(out_g, SHIFTS)]
    cs, act, wcat = forward(xs, wg, wu)
    packed, outgoing = middle(origin, at_row, gs, xs, wd, wcat, cs, act, copies)
    summed = lax.psum_scatter(packed, "dp", scatter_dimension=0, tiled=True)[0]
    ret = lax.all_to_all(outgoing, "expert", split_axis=0, concat_axis=0, tiled=True)
    grad_tokens = combine(ids_t, ret)
    grad_g, grad_u, grad_d = unpack(summed, width // copies, hidden, width, hidden // copies)
    return (grad_tokens, grad_g[None], grad_u[None], grad_d[None])


def solution(mesh):
    rows = P(("dp", "expert"), None)
    weights = P("expert", None, None)
    cut = P("expert", "dp", None)
    return jax.shard_map(
        shards,
        mesh=mesh,
        in_specs=(rows, rows, rows, rows, weights, weights, weights),
        out_specs=(rows, cut, cut, cut),
        check_vma=False,
    )
```

```python
import functools

import jax
import jax.numpy as jnp
from jax import lax
from jax.experimental import pallas as pl
from jax.experimental.pallas import tpu as pltpu
from jax.sharding import PartitionSpec as P

BF = jnp.bfloat16
F32 = jnp.float32
MIB = 1 << 20

MAIN = 32
REM = 4
PACK = 2 * (MAIN + REM)


SIDE = 4
CORES = 2
SHIFTS = [(d, f) for d in range(SIDE) for f in range(CORES)]
SPREAD = [(0, 0), (1, 0), (3, 0), (2, 0), (1, 1), (3, 1), (2, 1), (0, 1)]


def dot(a, b, ca=1, cb=0):
    return lax.dot_general(a, b, (((ca,), (cb,)), ((), ())), preferred_element_type=F32)


def iota(shape, dim):
    return lax.broadcasted_iota(jnp.int32, shape, dim)


def positions(ids, experts):
    top, toks = ids.shape
    ids_t = ids.astype(F32)
    ident = iota((experts, toks), 0).astype(F32)
    member = jnp.zeros((experts, toks), F32)
    for k in range(top):
        member = member + jnp.where(ids_t[k : k + 1, :] == ident, 1.0, 0.0)
    before = (iota((toks, toks), 0) < iota((toks, toks), 1)).astype(F32).astype(BF)
    pos = dot(member.astype(BF), before)
    return jnp.where(member > 0.5, pos, -1.0), ids_t, ident


def select(pos):
    experts, toks = pos.shape
    wide = pos[:, None, :]
    main = (wide == iota((experts, MAIN, toks), 1).astype(F32)).astype(F32)
    rest = (wide == (MAIN + iota((experts, 2 * REM, toks), 1) % REM).astype(F32)).astype(F32)
    return main.reshape(experts * MAIN, toks), rest.reshape(experts * 2 * REM, toks)


def is_left(rows, cols):
    return iota((rows, cols), 0) % (2 * REM) < REM


def prepare_kernel(ids_ref, gates_ref, tokens_hbm, grads_hbm, tokens_out, grads_out, extra_ref, sems):
    width = tokens_hbm.shape[1]
    copies = [
        pltpu.make_async_copy(tokens_hbm, tokens_out.at[:, :width], sems.at[0]),
        pltpu.make_async_copy(grads_hbm, grads_out.at[:, :width], sems.at[1]),
    ]
    for copy in copies:
        copy.start()
    pos, ids_t, ident = positions(ids_ref[...], 32)
    gates_t = gates_ref[...]
    weight = jnp.zeros(pos.shape, F32)
    for k in range(gates_t.shape[0]):
        weight = weight + jnp.where(ids_t[k : k + 1, :] == ident, gates_t[k : k + 1, :], 0.0)
    high = weight.astype(BF).astype(F32)
    mid = (weight - high).astype(BF).astype(F32)
    low = weight - high - mid
    extra_ref[...] = jnp.concatenate([pos, high, mid, low], axis=0).T.astype(BF)
    for n, dst in enumerate((tokens_out, grads_out)):
        copies.append(pltpu.make_async_copy(extra_ref, dst.at[:, width:], sems.at[2 + n]))
        copies[-1].start()
    for copy in copies:
        copy.wait()


HBM = pl.BlockSpec(memory_space=pltpu.HBM)
VMEM = pl.BlockSpec(memory_space=pltpu.VMEM)


def in_hbm(*arrays):
    return [pltpu.with_memory_space_constraint(a, pltpu.HBM) for a in arrays]


def prepare(ids, gates, tokens, grads):
    toks, width = tokens.shape
    shape = pltpu.HBM((toks, width + 128), BF)
    return pl.pallas_call(
        prepare_kernel,
        out_shape=(shape, shape),
        in_specs=[VMEM, VMEM, HBM, HBM],
        out_specs=(HBM, HBM),
        scratch_shapes=[pltpu.VMEM((toks, 128), BF), pltpu.SemaphoreType.DMA((4,))],
        compiler_params=pltpu.CompilerParams(vmem_limit_bytes=16 * MIB),
        cost_estimate=pl.CostEstimate(flops=1 << 20, bytes_accessed=2 * MIB, transcendentals=0),
        name="prepare",
    )(ids, gates, *in_hbm(tokens, grads))


def dispatch_kernel(scaled, per, wanted_ref, starts_ref, *refs):
    lines, pieces = 4, 5
    sources = refs[:pieces]
    count = 8 if scaled else 1
    outs = refs[pieces : pieces + count]
    data_ref, s_ref, out_ref, scale_ref, in_sems, out_sems = refs[pieces + count :]
    experts, rows, width = out_ref.shape
    toks = sources[0].shape[0]

    loads = []
    for k, (src, line, above) in enumerate(zip(sources, (0, 1, 2, 2, 3), (0, 0, 0, toks // 2, 0))):
        row = pl.multiple_of(starts_ref[line] + above, 16)
        loads.append(pltpu.make_async_copy(src, data_ref.at[pl.ds(row, src.shape[0]), :], in_sems.at[k]))
        loads[-1].start()
    for load in loads:
        load.wait()

    extra = data_ref[:, width:]
    wanted = wanted_ref[...]
    lane = iota(wanted.shape, 1)

    def column(piece):
        pick = (lane == wanted + piece * 32).astype(F32).astype(BF)
        return dot(pick, extra, 1, 1)

    pos = column(0)
    pair, some = rows // 2, lines * toks // 2
    for h in range(2):
        mine = slice(h * some, (h + 1) * some)
        first = (iota((experts, some), 1) // toks * per).astype(F32)
        target = jnp.where(pos[:, mine] >= 0.0, pos[:, mine] + first, -1.0)
        chosen = target[:, None, :] == iota((experts, pair, some), 1).astype(F32)
        chosen = chosen.astype(F32)
        s_ref[h] = chosen.reshape(experts * pair, some).astype(BF)
        if scaled:
            weight = (column(1) + (column(2) + column(3)))[:, mine]
            total = jnp.sum(chosen * weight[:, None, :], axis=2, keepdims=True)
            scale_ref[h] = jnp.broadcast_to(total, (experts, pair, 128)).reshape(experts * pair, 128)

    stores = []
    parts = 4
    columns = width // parts
    for c in range(parts):
        cols = slice(c * columns, (c + 1) * columns)
        for h in range(2):
            got = dot(s_ref[h], data_ref[h * some : (h + 1) * some, cols])
            if scaled:
                got = got * jnp.concatenate([scale_ref[h]] * (columns // 128), axis=1)
            out_ref[:, h * pair : (h + 1) * pair, cols] = got.astype(BF).reshape(experts, pair, columns)
        for k, out in enumerate(outs):
            here, there = (out_ref.at[k], out) if scaled else (out_ref, out)
            at = (slice(None),) * (len(there.shape) - 1) + (cols,)
            stores.append(pltpu.make_async_copy(here.at[at], there.at[at], out_sems.at[c * count + k]))
            stores[-1].start()
    for store in stores:
        store.wait()


def dispatch(wanted, starts, lines, scaled):
    toks, width = lines[0].shape[0], lines[0].shape[1] - 128
    per, experts = MAIN + REM, 8
    rows, all_toks = SIDE * per, SIDE * toks
    shapes = (pltpu.HBM((rows, width), BF),) * experts if scaled else (pltpu.HBM((experts, rows, width), BF),)
    return pl.pallas_call(
        functools.partial(dispatch_kernel, scaled, per),
        out_shape=shapes,
        in_specs=[VMEM, pl.BlockSpec(memory_space=pltpu.SMEM)] + [HBM] * len(lines),
        out_specs=(HBM,) * len(shapes),
        scratch_shapes=[
            pltpu.VMEM((all_toks, width + 128), BF),
            pltpu.VMEM((2, experts * rows // 2, all_toks // 2), BF),
            pltpu.VMEM((experts, rows, width), BF),
            pltpu.VMEM((2, experts * rows // 2, 128), F32),
            pltpu.SemaphoreType.DMA((len(lines),)),
            pltpu.SemaphoreType.DMA((4 * len(shapes),)),
        ],
        compiler_params=pltpu.CompilerParams(vmem_limit_bytes=32 * MIB),
        cost_estimate=pl.CostEstimate(
            flops=2 * experts * rows * all_toks * width, bytes_accessed=7 * MIB, transcendentals=0
        ),
        name="dispatch",
    )(wanted, starts, *in_hbm(*lines))


def regrouped(block):
    return block % 4 * 8 + block // 4 % 2 * 4 + block // 8


def forward_kernel(*refs):
    blocks, wg_hbm, wu_hbm = refs[:3]
    cs_ref, at_ref, wcat_ref = refs[3:6]
    x_ref, act_ref, turn_ref, sems = refs[6:]
    rows = blocks.shape[1]
    hidden = wg_hbm.shape[1]
    loads = [
        pltpu.make_async_copy(wg_hbm, wcat_ref.at[:, :hidden], sems.at[8]),
        pltpu.make_async_copy(wu_hbm, wcat_ref.at[:, hidden:], sems.at[9]),
    ]
    loads += [
        pltpu.make_async_copy(blocks.at[k], x_ref.at[k * rows : (k + 1) * rows, :], sems.at[k]) for k in range(8)
    ]
    for load in loads:
        load.start()
    loads[0].wait()
    loads[1].wait()
    parts = 4
    most = 8 // parts * rows
    for i in range(parts):
        for load in loads[2 + i * 8 // parts : 2 + (i + 1) * 8 // parts]:
            load.wait()
        some = slice(i * most, (i + 1) * most)
        pre = dot(x_ref[some, :], wcat_ref[...])
        gate, up = pre[:, :hidden], pre[:, hidden:]
        sigma = jax.nn.sigmoid(gate)
        silu = gate * sigma
        cs_ref[some, :hidden] = up * sigma * (1.0 + gate * (1.0 - sigma))
        cs_ref[some, hidden:] = silu
        act_ref[some, :] = silu * up
    per = MAIN + REM
    for b in range(32):
        to = regrouped(b)
        turn_ref[to * per : (to + 1) * per, :] = act_ref[b * per : (b + 1) * per, :]
    at_ref[...] = turn_ref[...].astype(BF).T


def forward(blocks, wg, wu):
    width, hidden = wg.shape
    rows = 8 * blocks.shape[1]
    return pl.pallas_call(
        forward_kernel,
        out_shape=(
            jax.ShapeDtypeStruct((rows, 2 * hidden), F32),
            jax.ShapeDtypeStruct((hidden, rows), BF),
            jax.ShapeDtypeStruct((width, 2 * hidden), BF),
        ),
        in_specs=[HBM] * 3,
        out_specs=(VMEM,) * 3,
        scratch_shapes=[
            pltpu.VMEM((rows, width), BF),
            pltpu.VMEM((rows, hidden), F32),
            pltpu.VMEM((rows, hidden), F32),
            pltpu.SemaphoreType.DMA((10,)),
        ],
        compiler_params=pltpu.CompilerParams(vmem_limit_bytes=20 * MIB),
        cost_estimate=pl.CostEstimate(
            flops=2 * rows * width * 2 * hidden, bytes_accessed=16 * MIB, transcendentals=rows * hidden
        ),
        name="forward",
    )(*in_hbm(blocks, wg, wu))


def middle_kernel(*refs):
    to_ref, at_row_ref, gs, xs = refs[0], refs[1], refs[2:10], refs[10]
    wd_ref, wcat_ref, cs_ref, at_ref = refs[11:15]
    packed_hbm, pair_hbm = refs[15:17]
    (g_ref, x_ref, raw_ref, turn_ref, d_ref, dt_ref, dm_ref, dr_ref, packed_ref,
     pair_ref, sems, out_sems) = refs[17:]
    rows = gs[0].shape[0]
    copies = packed_ref.shape[0]
    n, _, half = pair_ref.shape
    hidden, both = at_ref.shape[0], wcat_ref.shape[1]
    per_block = MAIN + REM

    def load(src, dst, sem):
        copy = pltpu.make_async_copy(src, dst, sems.at[sem])
        copy.start()
        return copy

    order = sorted(range(8), key=lambda k: SPREAD[k])
    g_in = [load(gs[k], g_ref.at[pl.ds(pl.multiple_of(at_row_ref[k], 16), rows), :], k) for k in order]
    x_in = [load(xs.at[k], x_ref.at[k * rows : (k + 1) * rows, :], 8 + k) for k in range(8)]

    parts = 2
    most = 8 // parts * rows
    for i in range(parts):
        for copy in g_in[i * 8 // parts : (i + 1) * 8 // parts]:
            copy.wait()
        some = slice(i * most, (i + 1) * most)
        raw_ref[some, :] = dot(g_ref[some, :], wd_ref[...], 1, 1)
    for b in range(n):
        to = regrouped(b)
        turn_ref[to * per_block : (to + 1) * per_block, :] = raw_ref[b * per_block : (b + 1) * per_block, :]
    for i in range(parts):
        some = slice(i * most, (i + 1) * most)
        d_act = turn_ref[some, :]
        grad = jnp.concatenate([d_act, d_act], axis=1) * cs_ref[some, :]
        d_ref[some, :] = grad
    dt_ref[...] = d_ref[...].astype(BF).T
    dr_ref[...] = jnp.zeros_like(dr_ref)
    for b in range(n):
        dm_ref[b * MAIN : (b + 1) * MAIN, :] = d_ref[b * per_block : b * per_block + MAIN, :].astype(BF)
        dr_ref[b * 2 * REM : b * 2 * REM + REM, :] = d_ref[b * per_block + MAIN : (b + 1) * per_block, :]

    for copy in x_in:
        copy.wait()
    tile = 256
    per = 2 * half // copies
    slab = hidden // copies
    base = both * per // 128
    for j in range(2 * half // tile):
        cols = slice(j * tile, (j + 1) * tile)
        into = dot(dt_ref[...], x_ref[:, cols]).astype(BF)
        down = dot(at_ref[...], g_ref[:, cols]).astype(BF)
        for q in range(tile // 128):
            at = j * tile // 128 + q
            owner, piece = at * 128 // per, at % (per // 128)
            part = into[:, q * 128 : (q + 1) * 128]
            packed_ref[owner, piece * both : (piece + 1) * both, :] = part
            part = down[:, q * 128 : (q + 1) * 128].reshape(copies, slab, 128)
            packed_ref[:, base + at * slab : base + (at + 1) * slab, :] = part
    packed_out = pltpu.make_async_copy(packed_ref, packed_hbm, out_sems.at[n])
    packed_out.start()

    sent = []
    parts = 4
    step = n // parts
    most, few = step * MAIN, step * 2 * REM
    for i in range(parts):
        main = dm_ref[i * most : (i + 1) * most, :]
        rest = dr_ref[i * few : (i + 1) * few, :]
        d_left = jnp.concatenate([main, rest.astype(BF)], axis=0)
        d_right = jnp.concatenate([main, pltpu.roll(rest, REM, 0).astype(BF)], axis=0)
        y_left = dot(d_left, wcat_ref[:half, :], 1, 1)
        y_right = dot(d_right, wcat_ref[half:, :], 1, 1)
        some = slice(i * step, (i + 1) * step)
        pair_ref[some, 0:MAIN, :] = y_left[:most].astype(BF).reshape(step, MAIN, half)
        pair_ref[some, MAIN : 2 * MAIN, :] = y_right[:most].astype(BF).reshape(step, MAIN, half)
        tail = (y_left[most:] + y_right[most:]).astype(BF)
        pair_ref[some, 2 * MAIN : PACK, :] = tail.reshape(step, 2 * REM, half)
        for b in range(i * step, (i + 1) * step):
            copy = pltpu.make_async_copy(pair_ref.at[b], pair_hbm.at[to_ref[b]], out_sems.at[b])
            copy.start()
            sent.append(copy)
    for copy in sent:
        copy.wait()
    packed_out.wait()


def middle(to, at_row, gs, xs, wd, wcat, cs, act, copies):
    hidden, width = wd.shape
    both, rows = cs.shape[1], cs.shape[0]
    n, half = to.shape[0], width // 2
    length = 3 * hidden * width // copies // 128
    smem = pl.BlockSpec(memory_space=pltpu.SMEM)
    return pl.pallas_call(
        middle_kernel,
        out_shape=(pltpu.HBM((copies, length, 128), BF), pltpu.HBM((n, PACK, half), BF)),
        in_specs=[smem] * 2 + [pl.BlockSpec(memory_space=pl.ANY)] * 9 + [VMEM] * 4,
        out_specs=(HBM,) * 2,
        scratch_shapes=[
            pltpu.VMEM((rows, width), BF),
            pltpu.VMEM((rows, width), BF),
            pltpu.VMEM((rows, hidden), F32),
            pltpu.VMEM((rows, hidden), F32),
            pltpu.VMEM((rows, both), F32),
            pltpu.VMEM((both, rows), BF),
            pltpu.VMEM((n * MAIN, both), BF),
            pltpu.VMEM((n * 2 * REM, both), F32),
            pltpu.VMEM((copies, length, 128), BF),
            pltpu.VMEM((n, PACK, half), BF),
            pltpu.SemaphoreType.DMA((16,)),
            pltpu.SemaphoreType.DMA((n + 1,)),
        ],
        compiler_params=pltpu.CompilerParams(vmem_limit_bytes=40 * MIB),
        cost_estimate=pl.CostEstimate(flops=2 * rows * width * 6 * hidden, bytes_accessed=28 * MIB, transcendentals=0),
        name="middle",
    )(to, at_row, *gs, xs, wd, wcat, cs, act)


def unpack_kernel(in_ref, gate_ref, up_ref, down_ref):
    per, hidden = gate_ref.shape
    slab = down_ref.shape[0]
    base = 2 * hidden * per // 128
    for q in range(per // 128):
        both = in_ref[q * 2 * hidden : (q + 1) * 2 * hidden, :].T
        gate_ref[q * 128 : (q + 1) * 128, :] = both[:, :hidden]
        up_ref[q * 128 : (q + 1) * 128, :] = both[:, hidden:]
    for q in range(down_ref.shape[1] // 128):
        down_ref[:, q * 128 : (q + 1) * 128] = in_ref[base + q * slab : base + (q + 1) * slab, :]


def unpack(summed, per, hidden, width, slab):
    vmem = pl.BlockSpec(memory_space=pltpu.VMEM)
    return pl.pallas_call(
        unpack_kernel,
        out_shape=(
            jax.ShapeDtypeStruct((per, hidden), BF),
            jax.ShapeDtypeStruct((per, hidden), BF),
            jax.ShapeDtypeStruct((slab, width), BF),
        ),
        in_specs=[vmem],
        out_specs=(vmem, vmem, vmem),
        cost_estimate=pl.CostEstimate(flops=0, bytes_accessed=2 * MIB, transcendentals=0),
        name="unpack",
    )(summed)


def combine_kernel(ids_ref, ret_ref, out_ref, main_ref, rest_ref):
    experts, _, cols = ret_ref.shape
    toks = out_ref.shape[0]
    half = out_ref.shape[1] // 2
    c = pl.program_id(0)

    @pl.when(c == 0)
    def _():
        pos, _, _ = positions(ids_ref[...], experts)
        main, rest = select(pos)
        left = is_left(*rest.shape)
        main_ref[...] = main.T.astype(BF)
        rest_ref[0] = jnp.where(left, rest, 0.0).T.astype(BF)
        rest_ref[1] = jnp.where(left, 0.0, rest).T.astype(BF)

    tail = ret_ref[:, 2 * MAIN : PACK, :].reshape(experts * 2 * REM, cols)
    for side in range(2):
        body = ret_ref[:, side * MAIN : (side + 1) * MAIN, :].reshape(experts * MAIN, cols)
        total = dot(main_ref[...], body) + dot(rest_ref[side], tail)
        out_ref[:, pl.ds(pl.multiple_of(side * half + c * cols, 128), cols)] = total.astype(BF)


def combine(ids, ret):
    experts, _, half = ret.shape
    toks = ids.shape[1]
    steps = 4
    cols = half // steps
    return pl.pallas_call(
        combine_kernel,
        out_shape=jax.ShapeDtypeStruct((toks, 2 * half), BF),
        grid=(steps,),
        in_specs=[
            pl.BlockSpec(ids.shape, lambda c: (0, 0)),
            pl.BlockSpec((experts, PACK, cols), lambda c: (0, 0, c)),
        ],
        out_specs=pl.BlockSpec((toks, 2 * half), lambda c: (0, 0)),
        scratch_shapes=[
            pltpu.VMEM((toks, experts * MAIN), BF),
            pltpu.VMEM((2, toks, experts * 2 * REM), BF),
        ],
        compiler_params=pltpu.CompilerParams(vmem_limit_bytes=24 * MIB),
        cost_estimate=pl.CostEstimate(flops=2 * 1280 * toks * 2 * half, bytes_accessed=6 * MIB, transcendentals=0),
        name="combine",
    )(ids, ret)


def place(x, y, core):
    return (x % SIDE * SIDE + y % SIDE) * CORES + core


def moved(value, dx, dy, flip):
    if dx == dy == flip == 0:
        return value
    pairs = []
    for x in range(SIDE):
        for y in range(SIDE):
            for core in range(CORES):
                pairs.append((place(x, y, core), place(x + dx, y + dy, core ^ flip)))
    return lax.ppermute(value, "expert", pairs)


def shards(tokens, grad_out, gates, expert_ids, w_gate, w_up, w_down):
    copies = lax.axis_size("dp")
    wg, wu, wd = w_gate[0], w_up[0], w_down[0]
    width, hidden = wg.shape
    me = lax.axis_index("expert")
    x, y, core = me // (SIDE * CORES), me // CORES % SIDE, me % CORES
    wide = lambda values: jnp.broadcast_to(jnp.stack(values).astype(jnp.int32)[:, None], (len(values), 128))
    along_y = wide([place(x, d, f) for d, f in SHIFTS])
    along_x = wide([place(x + d, y, core ^ f) for d, f in SPREAD])
    toks = tokens.shape[0]
    near = jnp.arange(SIDE, dtype=jnp.int32)
    starts_x = near * toks
    starts_g = (y - near + SIDE) % SIDE * toks
    origin = jnp.stack([place(x - d + SIDE, b, f) for b, f in SHIFTS for d in range(SIDE)]).astype(jnp.int32)
    at_row = jnp.stack([(d * CORES + (core ^ f)) * SIDE * (MAIN + REM) for d, f in SPREAD]).astype(jnp.int32)

    ids_t = expert_ids.T
    tokens, grad_out = prepare(ids_t, gates.T, tokens, grad_out)
    near_x, near_g = [tokens], [grad_out]
    for d in (1, SIDE - 1):
        near_x.append(moved(tokens, d, 0, 0))
        near_g.append(moved(grad_out, 0, d, 0))
    cut = toks // 2
    lines_x = [tokens, near_x[1], moved(near_x[1][:cut], 1, 0, 0), moved(near_x[2][cut:], SIDE - 1, 0, 0), near_x[2]]
    lines_g = [grad_out, near_g[1], moved(near_g[1][:cut], 0, 1, 0), moved(near_g[2][cut:], 0, SIDE - 1, 0), near_g[2]]
    lines_x, lines_g = lax.optimization_barrier((lines_x, lines_g))
    (out_x,) = dispatch(along_y, starts_x, lines_x, False)
    columns = [[place(a, b, f) for b in range(SIDE) for f in range(CORES)] for a in range(SIDE)]
    xs = lax.all_to_all(out_x, "expert", split_axis=0, concat_axis=0, axis_index_groups=columns, tiled=True)
    along_x, _ = lax.optimization_barrier((along_x, out_x))
    out_g = dispatch(along_x, starts_g, lines_g, True)
    gs = [moved(v, d, 0, f) for v, (d, f) in zip(out_g, SPREAD)]
    cs, act, wcat = forward(xs, wg, wu)
    packed, outgoing = middle(origin, at_row, gs, xs, wd, wcat, cs, act, copies)
    summed = lax.psum_scatter(packed, "dp", scatter_dimension=0, tiled=True)[0]
    ret = lax.all_to_all(outgoing, "expert", split_axis=0, concat_axis=0, tiled=True)
    grad_tokens = combine(ids_t, ret)
    grad_g, grad_u, grad_d = unpack(summed, width // copies, hidden, width, hidden // copies)
    return (grad_tokens, grad_g[None], grad_u[None], grad_d[None])


def solution(mesh):
    rows = P(("dp", "expert"), None)
    weights = P("expert", None, None)
    cut = P("expert", "dp", None)
    return jax.shard_map(
        shards,
        mesh=mesh,
        in_specs=(rows, rows, rows, rows, weights, weights, weights),
        out_specs=(rows, cut, cut, cut),
        check_vma=False,
    )
```

```python
import functools

import jax
import jax.numpy as jnp
from jax import lax
from jax.experimental import pallas as pl
from jax.experimental.pallas import tpu as pltpu
from jax.sharding import PartitionSpec as P

BF = jnp.bfloat16
F32 = jnp.float32
MIB = 1 << 20

MAIN = 32
REM = 4
PACK = 2 * (MAIN + REM)


SIDE = 4
CORES = 2
SHIFTS = [(d, f) for d in range(SIDE) for f in range(CORES)]
SPREAD = [(0, 0), (1, 0), (3, 0), (2, 0), (1, 1), (3, 1), (2, 1), (0, 1)]


def dot(a, b, ca=1, cb=0):
    return lax.dot_general(a, b, (((ca,), (cb,)), ((), ())), preferred_element_type=F32)


def iota(shape, dim):
    return lax.broadcasted_iota(jnp.int32, shape, dim)


def positions(ids, experts):
    top, toks = ids.shape
    ids_t = ids.astype(F32)
    ident = iota((experts, toks), 0).astype(F32)
    member = jnp.zeros((experts, toks), F32)
    for k in range(top):
        member = member + jnp.where(ids_t[k : k + 1, :] == ident, 1.0, 0.0)
    before = (iota((toks, toks), 0) < iota((toks, toks), 1)).astype(F32).astype(BF)
    pos = dot(member.astype(BF), before)
    return jnp.where(member > 0.5, pos, -1.0), ids_t, ident


def select(pos):
    experts, toks = pos.shape
    wide = pos[:, None, :]
    main = (wide == iota((experts, MAIN, toks), 1).astype(F32)).astype(F32)
    rest = (wide == (MAIN + iota((experts, 2 * REM, toks), 1) % REM).astype(F32)).astype(F32)
    return main.reshape(experts * MAIN, toks), rest.reshape(experts * 2 * REM, toks)


def is_left(rows, cols):
    return iota((rows, cols), 0) % (2 * REM) < REM


def prepare_kernel(ids_ref, gates_ref, tokens_hbm, grads_hbm, tokens_out, grads_out, row_ref, sems):
    width = tokens_hbm.shape[1]
    loads = [
        pltpu.make_async_copy(src, row_ref.at[n, :, :width], sems.at[n]) for n, src in enumerate((tokens_hbm, grads_hbm))
    ]
    for load in loads:
        load.start()
    pos, ids_t, ident = positions(ids_ref[...], 32)
    gates_t = gates_ref[...]
    weight = jnp.zeros(pos.shape, F32)
    for k in range(gates_t.shape[0]):
        weight = weight + jnp.where(ids_t[k : k + 1, :] == ident, gates_t[k : k + 1, :], 0.0)
    high = weight.astype(BF).astype(F32)
    mid = (weight - high).astype(BF).astype(F32)
    low = weight - high - mid
    extra = jnp.concatenate([pos, high, mid, low], axis=0).T.astype(BF)
    stores = []
    for n, dst in enumerate((tokens_out, grads_out)):
        row_ref[n, :, width:] = extra
        loads[n].wait()
        stores.append(pltpu.make_async_copy(row_ref.at[n], dst, sems.at[2 + n]))
        stores[-1].start()
    for store in stores:
        store.wait()


HBM = pl.BlockSpec(memory_space=pltpu.HBM)
VMEM = pl.BlockSpec(memory_space=pltpu.VMEM)


def in_hbm(*arrays):
    return [pltpu.with_memory_space_constraint(a, pltpu.HBM) for a in arrays]


def prepare(ids, gates, tokens, grads):
    toks, width = tokens.shape
    shape = pltpu.HBM((toks, width + 128), BF)
    return pl.pallas_call(
        prepare_kernel,
        out_shape=(shape, shape),
        in_specs=[VMEM, VMEM, HBM, HBM],
        out_specs=(HBM, HBM),
        scratch_shapes=[pltpu.VMEM((2, toks, width + 128), BF), pltpu.SemaphoreType.DMA((4,))],
        compiler_params=pltpu.CompilerParams(vmem_limit_bytes=16 * MIB),
        cost_estimate=pl.CostEstimate(flops=1 << 20, bytes_accessed=2 * MIB, transcendentals=0),
        name="prepare",
    )(ids, gates, *in_hbm(tokens, grads))


def dispatch_kernel(scaled, per, wanted_ref, starts_ref, *refs):
    lines, pieces = 4, 5
    sources = refs[:pieces]
    count = 8 if scaled else 1
    outs = refs[pieces : pieces + count]
    data_ref, s_ref, out_ref, scale_ref, in_sems, out_sems = refs[pieces + count :]
    experts, rows, width = out_ref.shape
    toks = sources[0].shape[0]

    loads = []
    for k, (src, line, above) in enumerate(zip(sources, (0, 1, 2, 2, 3), (0, 0, 0, toks // 2, 0))):
        row = pl.multiple_of(starts_ref[line] + above, 16)
        loads.append(pltpu.make_async_copy(src, data_ref.at[pl.ds(row, src.shape[0]), :], in_sems.at[k]))
        loads[-1].start()
    for load in loads:
        load.wait()

    extra = data_ref[:, width:]
    wanted = wanted_ref[...]
    lane = iota(wanted.shape, 1)

    def column(piece):
        pick = (lane == wanted + piece * 32).astype(F32).astype(BF)
        return dot(pick, extra, 1, 1)

    pos = column(0)
    pair, some = rows // 2, lines * toks // 2
    for h in range(2):
        mine = slice(h * some, (h + 1) * some)
        first = (iota((experts, some), 1) // toks * per).astype(F32)
        target = jnp.where(pos[:, mine] >= 0.0, pos[:, mine] + first, -1.0)
        chosen = target[:, None, :] == iota((experts, pair, some), 1).astype(F32)
        chosen = chosen.astype(F32)
        s_ref[h] = chosen.reshape(experts * pair, some).astype(BF)
        if scaled:
            weight = (column(1) + (column(2) + column(3)))[:, mine]
            total = jnp.sum(chosen * weight[:, None, :], axis=2, keepdims=True)
            scale_ref[h] = jnp.broadcast_to(total, (experts, pair, 128)).reshape(experts * pair, 128)

    stores = []
    parts = 4
    columns = width // parts
    for c in range(parts):
        cols = slice(c * columns, (c + 1) * columns)
        for h in range(2):
            got = dot(s_ref[h], data_ref[h * some : (h + 1) * some, cols])
            if scaled:
                got = got * jnp.concatenate([scale_ref[h]] * (columns // 128), axis=1)
            out_ref[:, h * pair : (h + 1) * pair, cols] = got.astype(BF).reshape(experts, pair, columns)
        for k, out in enumerate(outs):
            here, there = (out_ref.at[k], out) if scaled else (out_ref, out)
            at = (slice(None),) * (len(there.shape) - 1) + (cols,)
            stores.append(pltpu.make_async_copy(here.at[at], there.at[at], out_sems.at[c * count + k]))
            stores[-1].start()
    for store in stores:
        store.wait()


def dispatch(wanted, starts, lines, scaled):
    toks, width = lines[0].shape[0], lines[0].shape[1] - 128
    per, experts = MAIN + REM, 8
    rows, all_toks = SIDE * per, SIDE * toks
    shapes = (pltpu.HBM((rows, width), BF),) * experts if scaled else (pltpu.HBM((experts, rows, width), BF),)
    return pl.pallas_call(
        functools.partial(dispatch_kernel, scaled, per),
        out_shape=shapes,
        in_specs=[VMEM, pl.BlockSpec(memory_space=pltpu.SMEM)] + [HBM] * len(lines),
        out_specs=(HBM,) * len(shapes),
        scratch_shapes=[
            pltpu.VMEM((all_toks, width + 128), BF),
            pltpu.VMEM((2, experts * rows // 2, all_toks // 2), BF),
            pltpu.VMEM((experts, rows, width), BF),
            pltpu.VMEM((2, experts * rows // 2, 128), F32),
            pltpu.SemaphoreType.DMA((len(lines),)),
            pltpu.SemaphoreType.DMA((4 * len(shapes),)),
        ],
        compiler_params=pltpu.CompilerParams(vmem_limit_bytes=32 * MIB),
        cost_estimate=pl.CostEstimate(
            flops=2 * experts * rows * all_toks * width, bytes_accessed=7 * MIB, transcendentals=0
        ),
        name="dispatch",
    )(wanted, starts, *in_hbm(*lines))


def regrouped(block):
    return block % 4 * 8 + block // 4 % 2 * 4 + block // 8


def place_g(gs, at_row_ref, g_ref, sems):
    rows = gs[0].shape[0]
    copies = []
    for k in sorted(range(8), key=lambda k: SPREAD[k]):
        at = pl.ds(pl.multiple_of(at_row_ref[k], 16), rows)
        copies.append(pltpu.make_async_copy(gs[k], g_ref.at[at, :], sems.at[k]))
        copies[-1].start()
    return copies


def back_kernel(*refs):
    at_row_ref, gs, (wd_ref, wg_ref, wu_ref) = refs[0], refs[1:9], refs[9:12]
    out_ref, wcat_ref, g_ref, raw_ref, sems = refs[12:]
    hidden = wd_ref.shape[0]
    rows = gs[0].shape[0]
    copies = place_g(gs, at_row_ref, g_ref, sems)
    wcat_ref[:, :hidden] = wg_ref[...]
    wcat_ref[:, hidden:] = wu_ref[...]
    parts = 2
    most = 8 // parts * rows
    for i in range(parts):
        for copy in copies[i * 8 // parts : (i + 1) * 8 // parts]:
            copy.wait()
        some = slice(i * most, (i + 1) * most)
        raw_ref[some, :] = dot(g_ref[some, :], wd_ref[...], 1, 1)
    per = MAIN + REM
    for b in range(32):
        to = regrouped(b)
        out_ref[to * per : (to + 1) * per, :] = raw_ref[b * per : (b + 1) * per, :]


def back(at_row, gs, wd, wg, wu):
    hidden, width = wd.shape
    rows = 8 * gs[0].shape[0]
    smem = pl.BlockSpec(memory_space=pltpu.SMEM)
    return pl.pallas_call(
        back_kernel,
        out_shape=(
            jax.ShapeDtypeStruct((rows, hidden), F32),
            jax.ShapeDtypeStruct((width, 2 * hidden), BF),
        ),
        in_specs=[smem] + [pl.BlockSpec(memory_space=pl.ANY)] * 8 + [VMEM] * 3,
        out_specs=(VMEM, VMEM),
        scratch_shapes=[
            pltpu.VMEM((rows, width), BF),
            pltpu.VMEM((rows, hidden), F32),
            pltpu.SemaphoreType.DMA((8,)),
        ],
        compiler_params=pltpu.CompilerParams(vmem_limit_bytes=20 * MIB),
        cost_estimate=pl.CostEstimate(flops=2 * rows * width * hidden, bytes_accessed=12 * MIB, transcendentals=0),
        name="back",
    )(at_row, *gs, wd, wg, wu)


def middle_kernel(*refs):
    to_ref, at_row_ref, gs, xs = refs[0], refs[1], refs[2:10], refs[10]
    back_ref, wcat_ref, packed_hbm, pair_hbm = refs[11:15]
    (g_ref, x_ref, act_ref, turn_ref, d_ref, dt_ref, at_ref, dm_ref, dr_ref, packed_ref,
     pair_ref, sems, out_sems) = refs[15:]
    rows = gs[0].shape[0]
    copies = packed_ref.shape[0]
    n, _, half = pair_ref.shape
    both = wcat_ref.shape[1]
    hidden = both // 2
    per_block = MAIN + REM

    x_in = [
        pltpu.make_async_copy(xs.at[k], x_ref.at[k * rows : (k + 1) * rows, :], sems.at[8 + k]) for k in range(8)
    ]
    for copy in x_in:
        copy.start()
    g_in = place_g(gs, at_row_ref, g_ref, sems)

    parts = 4
    most = 8 // parts * rows
    for i in range(parts):
        for copy in x_in[i * 8 // parts : (i + 1) * 8 // parts]:
            copy.wait()
        some = slice(i * most, (i + 1) * most)
        pre = dot(x_ref[some, :], wcat_ref[...])
        gate, up = pre[:, :hidden], pre[:, hidden:]
        sigma = jax.nn.sigmoid(gate)
        silu = gate * sigma
        d_act = back_ref[some, :]
        d_ref[some, :hidden] = d_act * up * sigma * (1.0 + gate * (1.0 - sigma))
        d_ref[some, hidden:] = d_act * silu
        act_ref[some, :] = silu * up
    dr_ref[...] = jnp.zeros_like(dr_ref)
    for b in range(n):
        to = regrouped(b)
        turn_ref[to * per_block : (to + 1) * per_block, :] = act_ref[b * per_block : (b + 1) * per_block, :]
        dm_ref[b * MAIN : (b + 1) * MAIN, :] = d_ref[b * per_block : b * per_block + MAIN, :].astype(BF)
        dr_ref[b * 2 * REM : b * 2 * REM + REM, :] = d_ref[b * per_block + MAIN : (b + 1) * per_block, :]
    dt_ref[...] = d_ref[...].astype(BF).T
    at_ref[...] = turn_ref[...].astype(BF).T

    for copy in g_in:
        copy.wait()
    tile = 256
    per = 2 * half // copies
    slab = hidden // copies
    base = both * per // 128
    for j in range(2 * half // tile):
        cols = slice(j * tile, (j + 1) * tile)
        into = dot(dt_ref[...], x_ref[:, cols]).astype(BF)
        down = dot(at_ref[...], g_ref[:, cols]).astype(BF)
        for q in range(tile // 128):
            at = j * tile // 128 + q
            owner, piece = at * 128 // per, at % (per // 128)
            part = into[:, q * 128 : (q + 1) * 128]
            packed_ref[owner, piece * both : (piece + 1) * both, :] = part
            part = down[:, q * 128 : (q + 1) * 128].reshape(copies, slab, 128)
            packed_ref[:, base + at * slab : base + (at + 1) * slab, :] = part
    packed_out = pltpu.make_async_copy(packed_ref, packed_hbm, out_sems.at[n])
    packed_out.start()

    sent = []
    step = n // parts
    most, few = step * MAIN, step * 2 * REM
    for i in range(parts):
        main = dm_ref[i * most : (i + 1) * most, :]
        rest = dr_ref[i * few : (i + 1) * few, :]
        d_left = jnp.concatenate([main, rest.astype(BF)], axis=0)
        d_right = jnp.concatenate([main, pltpu.roll(rest, REM, 0).astype(BF)], axis=0)
        y_left = dot(d_left, wcat_ref[:half, :], 1, 1)
        y_right = dot(d_right, wcat_ref[half:, :], 1, 1)
        some = slice(i * step, (i + 1) * step)
        pair_ref[some, 0:MAIN, :] = y_left[:most].astype(BF).reshape(step, MAIN, half)
        pair_ref[some, MAIN : 2 * MAIN, :] = y_right[:most].astype(BF).reshape(step, MAIN, half)
        tail = (y_left[most:] + y_right[most:]).astype(BF)
        pair_ref[some, 2 * MAIN : PACK, :] = tail.reshape(step, 2 * REM, half)
        for b in range(i * step, (i + 1) * step):
            copy = pltpu.make_async_copy(pair_ref.at[b], pair_hbm.at[to_ref[b]], out_sems.at[b])
            copy.start()
            sent.append(copy)
    for copy in sent:
        copy.wait()
    packed_out.wait()


def middle(to, at_row, gs, xs, back_x, wcat, copies):
    width, both = wcat.shape
    rows, hidden = back_x.shape
    n, half = to.shape[0], width // 2
    length = 3 * hidden * width // copies // 128
    smem = pl.BlockSpec(memory_space=pltpu.SMEM)
    return pl.pallas_call(
        middle_kernel,
        out_shape=(pltpu.HBM((copies, length, 128), BF), pltpu.HBM((n, PACK, half), BF)),
        in_specs=[smem] * 2 + [pl.BlockSpec(memory_space=pl.ANY)] * 9 + [VMEM] * 2,
        out_specs=(HBM,) * 2,
        scratch_shapes=[
            pltpu.VMEM((rows, width), BF),
            pltpu.VMEM((rows, width), BF),
            pltpu.VMEM((rows, hidden), F32),
            pltpu.VMEM((rows, hidden), F32),
            pltpu.VMEM((rows, both), F32),
            pltpu.VMEM((both, rows), BF),
            pltpu.VMEM((hidden, rows), BF),
            pltpu.VMEM((n * MAIN, both), BF),
            pltpu.VMEM((n * 2 * REM, both), F32),
            pltpu.VMEM((copies, length, 128), BF),
            pltpu.VMEM((n, PACK, half), BF),
            pltpu.SemaphoreType.DMA((16,)),
            pltpu.SemaphoreType.DMA((n + 1,)),
        ],
        compiler_params=pltpu.CompilerParams(vmem_limit_bytes=42 * MIB),
        cost_estimate=pl.CostEstimate(
            flops=2 * rows * width * 7 * hidden, bytes_accessed=24 * MIB, transcendentals=rows * hidden
        ),
        name="middle",
    )(to, at_row, *gs, xs, back_x, wcat)


def unpack_kernel(in_ref, gate_ref, up_ref, down_ref):
    per, hidden = gate_ref.shape
    slab = down_ref.shape[0]
    base = 2 * hidden * per // 128
    for q in range(per // 128):
        both = in_ref[q * 2 * hidden : (q + 1) * 2 * hidden, :].T
        gate_ref[q * 128 : (q + 1) * 128, :] = both[:, :hidden]
        up_ref[q * 128 : (q + 1) * 128, :] = both[:, hidden:]
    for q in range(down_ref.shape[1] // 128):
        down_ref[:, q * 128 : (q + 1) * 128] = in_ref[base + q * slab : base + (q + 1) * slab, :]


def unpack(summed, per, hidden, width, slab):
    vmem = pl.BlockSpec(memory_space=pltpu.VMEM)
    return pl.pallas_call(
        unpack_kernel,
        out_shape=(
            jax.ShapeDtypeStruct((per, hidden), BF),
            jax.ShapeDtypeStruct((per, hidden), BF),
            jax.ShapeDtypeStruct((slab, width), BF),
        ),
        in_specs=[vmem],
        out_specs=(vmem, vmem, vmem),
        cost_estimate=pl.CostEstimate(flops=0, bytes_accessed=2 * MIB, transcendentals=0),
        name="unpack",
    )(summed)


def combine_kernel(ids_ref, ret_ref, out_ref, main_ref, rest_ref):
    experts, _, cols = ret_ref.shape
    toks = out_ref.shape[0]
    half = out_ref.shape[1] // 2
    c = pl.program_id(0)

    @pl.when(c == 0)
    def _():
        pos, _, _ = positions(ids_ref[...], experts)
        main, rest = select(pos)
        left = is_left(*rest.shape)
        main_ref[...] = main.T.astype(BF)
        rest_ref[0] = jnp.where(left, rest, 0.0).T.astype(BF)
        rest_ref[1] = jnp.where(left, 0.0, rest).T.astype(BF)

    tail = ret_ref[:, 2 * MAIN : PACK, :].reshape(experts * 2 * REM, cols)
    for side in range(2):
        body = ret_ref[:, side * MAIN : (side + 1) * MAIN, :].reshape(experts * MAIN, cols)
        total = dot(main_ref[...], body) + dot(rest_ref[side], tail)
        out_ref[:, pl.ds(pl.multiple_of(side * half + c * cols, 128), cols)] = total.astype(BF)


def combine(ids, ret):
    experts, _, half = ret.shape
    toks = ids.shape[1]
    steps = 4
    cols = half // steps
    return pl.pallas_call(
        combine_kernel,
        out_shape=jax.ShapeDtypeStruct((toks, 2 * half), BF),
        grid=(steps,),
        in_specs=[
            pl.BlockSpec(ids.shape, lambda c: (0, 0)),
            pl.BlockSpec((experts, PACK, cols), lambda c: (0, 0, c)),
        ],
        out_specs=pl.BlockSpec((toks, 2 * half), lambda c: (0, 0)),
        scratch_shapes=[
            pltpu.VMEM((toks, experts * MAIN), BF),
            pltpu.VMEM((2, toks, experts * 2 * REM), BF),
        ],
        compiler_params=pltpu.CompilerParams(vmem_limit_bytes=24 * MIB),
        cost_estimate=pl.CostEstimate(flops=2 * 1280 * toks * 2 * half, bytes_accessed=6 * MIB, transcendentals=0),
        name="combine",
    )(ids, ret)


def place(x, y, core):
    return (x % SIDE * SIDE + y % SIDE) * CORES + core


def moved(value, dx, dy, flip):
    if dx == dy == flip == 0:
        return value
    pairs = []
    for x in range(SIDE):
        for y in range(SIDE):
            for core in range(CORES):
                pairs.append((place(x, y, core), place(x + dx, y + dy, core ^ flip)))
    return lax.ppermute(value, "expert", pairs)


def shards(tokens, grad_out, gates, expert_ids, w_gate, w_up, w_down):
    copies = lax.axis_size("dp")
    wg, wu, wd = w_gate[0], w_up[0], w_down[0]
    width, hidden = wg.shape
    me = lax.axis_index("expert")
    x, y, core = me // (SIDE * CORES), me // CORES % SIDE, me % CORES
    wide = lambda values: jnp.broadcast_to(jnp.stack(values).astype(jnp.int32)[:, None], (len(values), 128))
    along_y = wide([place(x, d, f) for d, f in SHIFTS])
    along_x = wide([place(x + d, y, core ^ f) for d, f in SPREAD])
    toks = tokens.shape[0]
    near = jnp.arange(SIDE, dtype=jnp.int32)
    starts_x = near * toks
    starts_g = (y - near + SIDE) % SIDE * toks
    origin = jnp.stack([place(x - d + SIDE, b, f) for b, f in SHIFTS for d in range(SIDE)]).astype(jnp.int32)
    at_row = jnp.stack([(d * CORES + (core ^ f)) * SIDE * (MAIN + REM) for d, f in SPREAD]).astype(jnp.int32)

    ids_t = expert_ids.T
    tokens, grad_out = prepare(ids_t, gates.T, tokens, grad_out)
    near_x, near_g = [tokens], [grad_out]
    for d in (1, SIDE - 1):
        near_x.append(moved(tokens, d, 0, 0))
        near_g.append(moved(grad_out, 0, d, 0))
    cut = toks // 2
    lines_x = [tokens, near_x[1], moved(near_x[1][:cut], 1, 0, 0), moved(near_x[2][cut:], SIDE - 1, 0, 0), near_x[2]]
    lines_g = [grad_out, near_g[1], moved(near_g[1][:cut], 0, 1, 0), moved(near_g[2][cut:], 0, SIDE - 1, 0), near_g[2]]
    lines_x, lines_g = lax.optimization_barrier((lines_x, lines_g))
    (out_x,) = dispatch(along_y, starts_x, lines_x, False)
    columns = [[place(a, b, f) for b in range(SIDE) for f in range(CORES)] for a in range(SIDE)]
    xs = lax.all_to_all(out_x, "expert", split_axis=0, concat_axis=0, axis_index_groups=columns, tiled=True)
    along_x, _ = lax.optimization_barrier((along_x, out_x))
    out_g = dispatch(along_x, starts_g, lines_g, True)
    gs = [moved(v, d, 0, f) for v, (d, f) in zip(out_g, SPREAD)]
    back_x, wcat = back(at_row, gs, wd, wg, wu)
    packed, outgoing = middle(origin, at_row, gs, xs, back_x, wcat, copies)
    summed = lax.psum_scatter(packed, "dp", scatter_dimension=0, tiled=True)[0]
    ret = lax.all_to_all(outgoing, "expert", split_axis=0, concat_axis=0, tiled=True)
    grad_tokens = combine(ids_t, ret)
    grad_g, grad_u, grad_d = unpack(summed, width // copies, hidden, width, hidden // copies)
    return (grad_tokens, grad_g[None], grad_u[None], grad_d[None])


def solution(mesh):
    rows = P(("dp", "expert"), None)
    weights = P("expert", None, None)
    cut = P("expert", "dp", None)
    return jax.shard_map(
        shards,
        mesh=mesh,
        in_specs=(rows, rows, rows, rows, weights, weights, weights),
        out_specs=(rows, cut, cut, cut),
        check_vma=False,
    )
```

```python
import functools

import jax
import jax.numpy as jnp
from jax import lax
from jax.experimental import pallas as pl
from jax.experimental.pallas import tpu as pltpu
from jax.sharding import PartitionSpec as P

BF = jnp.bfloat16
F32 = jnp.float32
MIB = 1 << 20

MAIN = 32
REM = 4
PACK = 2 * (MAIN + REM)


SIDE = 4
CORES = 2
SHIFTS = [(d, f) for d in range(SIDE) for f in range(CORES)]
SPREAD = [(0, 0), (1, 0), (3, 0), (2, 0), (1, 1), (3, 1), (2, 1), (0, 1)]


def dot(a, b, ca=1, cb=0):
    return lax.dot_general(a, b, (((ca,), (cb,)), ((), ())), preferred_element_type=F32)


def iota(shape, dim):
    return lax.broadcasted_iota(jnp.int32, shape, dim)


def positions(ids, experts):
    top, toks = ids.shape
    ids_t = ids.astype(F32)
    ident = iota((experts, toks), 0).astype(F32)
    member = jnp.zeros((experts, toks), F32)
    for k in range(top):
        member = member + jnp.where(ids_t[k : k + 1, :] == ident, 1.0, 0.0)
    before = (iota((toks, toks), 0) < iota((toks, toks), 1)).astype(F32).astype(BF)
    pos = dot(member.astype(BF), before)
    return jnp.where(member > 0.5, pos, -1.0), ids_t, ident


def select(pos):
    experts, toks = pos.shape
    wide = pos[:, None, :]
    main = (wide == iota((experts, MAIN, toks), 1).astype(F32)).astype(F32)
    rest = (wide == (MAIN + iota((experts, 2 * REM, toks), 1) % REM).astype(F32)).astype(F32)
    return main.reshape(experts * MAIN, toks), rest.reshape(experts * 2 * REM, toks)


def is_left(rows, cols):
    return iota((rows, cols), 0) % (2 * REM) < REM


def prepare_kernel(ids_hbm, gates_hbm, tokens_hbm, grads_hbm, tokens_out, grads_out, row_ref, ids_ref, gates_ref, sems):
    width = tokens_hbm.shape[1]
    loads = [
        pltpu.make_async_copy(src, row_ref.at[n, :, :width], sems.at[n]) for n, src in enumerate((tokens_hbm, grads_hbm))
    ]
    small = [pltpu.make_async_copy(ids_hbm, ids_ref, sems.at[4]), pltpu.make_async_copy(gates_hbm, gates_ref, sems.at[5])]
    for load in small + loads:
        load.start()
    for load in small:
        load.wait()
    pos, ids_t, ident = positions(ids_ref[...], 32)
    gates_t = gates_ref[...]
    weight = jnp.zeros(pos.shape, F32)
    for k in range(gates_t.shape[0]):
        weight = weight + jnp.where(ids_t[k : k + 1, :] == ident, gates_t[k : k + 1, :], 0.0)
    high = weight.astype(BF).astype(F32)
    mid = (weight - high).astype(BF).astype(F32)
    low = weight - high - mid
    extra = jnp.concatenate([pos, high, mid, low], axis=0).T.astype(BF)
    stores = []
    for n, dst in enumerate((tokens_out, grads_out)):
        row_ref[n, :, width:] = extra
        loads[n].wait()
        stores.append(pltpu.make_async_copy(row_ref.at[n], dst, sems.at[2 + n]))
        stores[-1].start()
    for store in stores:
        store.wait()


HBM = pl.BlockSpec(memory_space=pltpu.HBM)
VMEM = pl.BlockSpec(memory_space=pltpu.VMEM)


def in_hbm(*arrays):
    return [pltpu.with_memory_space_constraint(a, pltpu.HBM) for a in arrays]


def prepare(ids, gates, tokens, grads):
    toks, width = tokens.shape
    shape = pltpu.HBM((toks, width + 128), BF)
    return pl.pallas_call(
        prepare_kernel,
        out_shape=(shape, shape),
        in_specs=[HBM] * 4,
        out_specs=(HBM, HBM),
        scratch_shapes=[
            pltpu.VMEM((2, toks, width + 128), BF),
            pltpu.VMEM(ids.shape, ids.dtype),
            pltpu.VMEM(gates.shape, F32),
            pltpu.SemaphoreType.DMA((6,)),
        ],
        compiler_params=pltpu.CompilerParams(vmem_limit_bytes=16 * MIB),
        cost_estimate=pl.CostEstimate(flops=1 << 20, bytes_accessed=2 * MIB, transcendentals=0),
        name="prepare",
    )(*in_hbm(ids, gates, tokens, grads))


def dispatch_kernel(scaled, per, wanted_ref, starts_ref, *refs):
    lines, pieces = 4, 5
    sources = refs[:pieces]
    count = 8 if scaled else 1
    outs = refs[pieces : pieces + count]
    data_ref, s_ref, out_ref, scale_ref, in_sems, out_sems = refs[pieces + count :]
    experts, rows, width = out_ref.shape
    toks = sources[0].shape[0]

    loads = []
    for k, (src, line, above) in enumerate(zip(sources, (0, 1, 2, 2, 3), (0, 0, 0, toks // 2, 0))):
        row = pl.multiple_of(starts_ref[line] + above, 16)
        loads.append(pltpu.make_async_copy(src, data_ref.at[pl.ds(row, src.shape[0]), :], in_sems.at[k]))
        loads[-1].start()
    for load in loads:
        load.wait()

    extra = data_ref[:, width:]
    wanted = wanted_ref[...]
    lane = iota(wanted.shape, 1)

    def column(piece):
        pick = (lane == wanted + piece * 32).astype(F32).astype(BF)
        return dot(pick, extra, 1, 1)

    pos = column(0)
    pair, some = rows // 2, lines * toks // 2
    for h in range(2):
        mine = slice(h * some, (h + 1) * some)
        first = (iota((experts, some), 1) // toks * per).astype(F32)
        target = jnp.where(pos[:, mine] >= 0.0, pos[:, mine] + first, -1.0)
        chosen = target[:, None, :] == iota((experts, pair, some), 1).astype(F32)
        chosen = chosen.astype(F32)
        s_ref[h] = chosen.reshape(experts * pair, some).astype(BF)
        if scaled:
            weight = (column(1) + (column(2) + column(3)))[:, mine]
            total = jnp.sum(chosen * weight[:, None, :], axis=2, keepdims=True)
            scale_ref[h] = jnp.broadcast_to(total, (experts, pair, 128)).reshape(experts * pair, 128)

    stores = []
    parts = 4
    columns = width // parts
    for c in range(parts):
        cols = slice(c * columns, (c + 1) * columns)
        for h in range(2):
            got = dot(s_ref[h], data_ref[h * some : (h + 1) * some, cols])
            if scaled:
                got = got * jnp.concatenate([scale_ref[h]] * (columns // 128), axis=1)
            out_ref[:, h * pair : (h + 1) * pair, cols] = got.astype(BF).reshape(experts, pair, columns)
        for k, out in enumerate(outs):
            here, there = (out_ref.at[k], out) if scaled else (out_ref, out)
            at = (slice(None),) * (len(there.shape) - 1) + (cols,)
            stores.append(pltpu.make_async_copy(here.at[at], there.at[at], out_sems.at[c * count + k]))
            stores[-1].start()
    for store in stores:
        store.wait()


def dispatch(wanted, starts, lines, scaled):
    toks, width = lines[0].shape[0], lines[0].shape[1] - 128
    per, experts = MAIN + REM, 8
    rows, all_toks = SIDE * per, SIDE * toks
    shapes = (pltpu.HBM((rows, width), BF),) * experts if scaled else (pltpu.HBM((experts, rows, width), BF),)
    return pl.pallas_call(
        functools.partial(dispatch_kernel, scaled, per),
        out_shape=shapes,
        in_specs=[VMEM, pl.BlockSpec(memory_space=pltpu.SMEM)] + [HBM] * len(lines),
        out_specs=(HBM,) * len(shapes),
        scratch_shapes=[
            pltpu.VMEM((all_toks, width + 128), BF),
            pltpu.VMEM((2, experts * rows // 2, all_toks // 2), BF),
            pltpu.VMEM((experts, rows, width), BF),
            pltpu.VMEM((2, experts * rows // 2, 128), F32),
            pltpu.SemaphoreType.DMA((len(lines),)),
            pltpu.SemaphoreType.DMA((4 * len(shapes),)),
        ],
        compiler_params=pltpu.CompilerParams(vmem_limit_bytes=32 * MIB),
        cost_estimate=pl.CostEstimate(
            flops=2 * experts * rows * all_toks * width, bytes_accessed=7 * MIB, transcendentals=0
        ),
        name="dispatch",
    )(wanted, starts, *in_hbm(*lines))


def regrouped(block):
    return block % 4 * 8 + block // 4 % 2 * 4 + block // 8


def forward_kernel(*refs):
    blocks, wg_hbm, wu_hbm = refs[:3]
    cs_ref, at_ref, wcat_ref = refs[3:6]
    x_ref, act_ref, turn_ref, sems = refs[6:]
    rows = blocks.shape[1]
    hidden = wg_hbm.shape[1]
    loads = [
        pltpu.make_async_copy(wg_hbm, wcat_ref.at[:, :hidden], sems.at[8]),
        pltpu.make_async_copy(wu_hbm, wcat_ref.at[:, hidden:], sems.at[9]),
    ]
    loads += [
        pltpu.make_async_copy(blocks.at[k], x_ref.at[k * rows : (k + 1) * rows, :], sems.at[k]) for k in range(8)
    ]
    for load in loads:
        load.start()
    loads[0].wait()
    loads[1].wait()
    parts = 4
    most = 8 // parts * rows
    for i in range(parts):
        for load in loads[2 + i * 8 // parts : 2 + (i + 1) * 8 // parts]:
            load.wait()
        some = slice(i * most, (i + 1) * most)
        pre = dot(x_ref[some, :], wcat_ref[...])
        gate, up = pre[:, :hidden], pre[:, hidden:]
        sigma = jax.nn.sigmoid(gate)
        silu = gate * sigma
        cs_ref[some, :hidden] = up * sigma * (1.0 + gate * (1.0 - sigma))
        cs_ref[some, hidden:] = silu
        act_ref[some, :] = silu * up
    per = MAIN + REM
    for b in range(32):
        to = regrouped(b)
        turn_ref[to * per : (to + 1) * per, :] = act_ref[b * per : (b + 1) * per, :]
    at_ref[...] = turn_ref[...].astype(BF).T


def forward(blocks, wg, wu):
    width, hidden = wg.shape
    rows = 8 * blocks.shape[1]
    return pl.pallas_call(
        forward_kernel,
        out_shape=(
            jax.ShapeDtypeStruct((rows, 2 * hidden), F32),
            jax.ShapeDtypeStruct((hidden, rows), BF),
            jax.ShapeDtypeStruct((width, 2 * hidden), BF),
        ),
        in_specs=[HBM] * 3,
        out_specs=(VMEM,) * 3,
        scratch_shapes=[
            pltpu.VMEM((rows, width), BF),
            pltpu.VMEM((rows, hidden), F32),
            pltpu.VMEM((rows, hidden), F32),
            pltpu.SemaphoreType.DMA((10,)),
        ],
        compiler_params=pltpu.CompilerParams(vmem_limit_bytes=20 * MIB),
        cost_estimate=pl.CostEstimate(
            flops=2 * rows * width * 2 * hidden, bytes_accessed=16 * MIB, transcendentals=rows * hidden
        ),
        name="forward",
    )(*in_hbm(blocks, wg, wu))


def middle_kernel(*refs):
    to_ref, at_row_ref, gs, xs = refs[0], refs[1], refs[2:10], refs[10]
    wd_ref, wcat_ref, cs_ref, at_ref = refs[11:15]
    packed_hbm, pair_hbm = refs[15:17]
    (g_ref, x_ref, raw_ref, turn_ref, d_ref, dt_ref, dm_ref, dr_ref, packed_ref,
     pair_ref, sems, out_sems) = refs[17:]
    rows = gs[0].shape[0]
    copies = packed_ref.shape[0]
    n, _, half = pair_ref.shape
    hidden, both = at_ref.shape[0], wcat_ref.shape[1]
    per_block = MAIN + REM

    def load(src, dst, sem):
        copy = pltpu.make_async_copy(src, dst, sems.at[sem])
        copy.start()
        return copy

    order = sorted(range(8), key=lambda k: SPREAD[k])
    g_in = [load(gs[k], g_ref.at[pl.ds(pl.multiple_of(at_row_ref[k], 16), rows), :], k) for k in order]
    x_in = [load(xs.at[k], x_ref.at[k * rows : (k + 1) * rows, :], 8 + k) for k in range(8)]

    parts = 2
    most = 8 // parts * rows
    for i in range(parts):
        for copy in g_in[i * 8 // parts : (i + 1) * 8 // parts]:
            copy.wait()
        some = slice(i * most, (i + 1) * most)
        raw_ref[some, :] = dot(g_ref[some, :], wd_ref[...], 1, 1)
    for b in range(n):
        to = regrouped(b)
        turn_ref[to * per_block : (to + 1) * per_block, :] = raw_ref[b * per_block : (b + 1) * per_block, :]
    for i in range(parts):
        some = slice(i * most, (i + 1) * most)
        d_act = turn_ref[some, :]
        grad = jnp.concatenate([d_act, d_act], axis=1) * cs_ref[some, :]
        d_ref[some, :] = grad
    dt_ref[...] = d_ref[...].astype(BF).T
    dr_ref[...] = jnp.zeros_like(dr_ref)
    for b in range(n):
        dm_ref[b * MAIN : (b + 1) * MAIN, :] = d_ref[b * per_block : b * per_block + MAIN, :].astype(BF)
        dr_ref[b * 2 * REM : b * 2 * REM + REM, :] = d_ref[b * per_block + MAIN : (b + 1) * per_block, :]

    for copy in x_in:
        copy.wait()
    tile = 256
    per = 2 * half // copies
    slab = hidden // copies
    base = both * per // 128
    for j in range(2 * half // tile):
        cols = slice(j * tile, (j + 1) * tile)
        into = dot(dt_ref[...], x_ref[:, cols]).astype(BF)
        down = dot(at_ref[...], g_ref[:, cols]).astype(BF)
        for q in range(tile // 128):
            at = j * tile // 128 + q
            owner, piece = at * 128 // per, at % (per // 128)
            part = into[:, q * 128 : (q + 1) * 128]
            packed_ref[owner, piece * both : (piece + 1) * both, :] = part
            part = down[:, q * 128 : (q + 1) * 128].reshape(copies, slab, 128)
            packed_ref[:, base + at * slab : base + (at + 1) * slab, :] = part
    packed_out = pltpu.make_async_copy(packed_ref, packed_hbm, out_sems.at[n])
    packed_out.start()

    sent = []
    parts = 4
    step = n // parts
    most, few = step * MAIN, step * 2 * REM
    for i in range(parts):
        main = dm_ref[i * most : (i + 1) * most, :]
        rest = dr_ref[i * few : (i + 1) * few, :]
        d_left = jnp.concatenate([main, rest.astype(BF)], axis=0)
        d_right = jnp.concatenate([main, pltpu.roll(rest, REM, 0).astype(BF)], axis=0)
        y_left = dot(d_left, wcat_ref[:half, :], 1, 1)
        y_right = dot(d_right, wcat_ref[half:, :], 1, 1)
        some = slice(i * step, (i + 1) * step)
        pair_ref[some, 0:MAIN, :] = y_left[:most].astype(BF).reshape(step, MAIN, half)
        pair_ref[some, MAIN : 2 * MAIN, :] = y_right[:most].astype(BF).reshape(step, MAIN, half)
        tail = (y_left[most:] + y_right[most:]).astype(BF)
        pair_ref[some, 2 * MAIN : PACK, :] = tail.reshape(step, 2 * REM, half)
        for b in range(i * step, (i + 1) * step):
            copy = pltpu.make_async_copy(pair_ref.at[b], pair_hbm.at[to_ref[b]], out_sems.at[b])
            copy.start()
            sent.append(copy)
    for copy in sent:
        copy.wait()
    packed_out.wait()


def middle(to, at_row, gs, xs, wd, wcat, cs, act, copies):
    hidden, width = wd.shape
    both, rows = cs.shape[1], cs.shape[0]
    n, half = to.shape[0], width // 2
    length = 3 * hidden * width // copies // 128
    smem = pl.BlockSpec(memory_space=pltpu.SMEM)
    return pl.pallas_call(
        middle_kernel,
        out_shape=(pltpu.HBM((copies, length, 128), BF), pltpu.HBM((n, PACK, half), BF)),
        in_specs=[smem] * 2 + [pl.BlockSpec(memory_space=pl.ANY)] * 9 + [VMEM] * 4,
        out_specs=(HBM,) * 2,
        scratch_shapes=[
            pltpu.VMEM((rows, width), BF),
            pltpu.VMEM((rows, width), BF),
            pltpu.VMEM((rows, hidden), F32),
            pltpu.VMEM((rows, hidden), F32),
            pltpu.VMEM((rows, both), F32),
            pltpu.VMEM((both, rows), BF),
            pltpu.VMEM((n * MAIN, both), BF),
            pltpu.VMEM((n * 2 * REM, both), F32),
            pltpu.VMEM((copies, length, 128), BF),
            pltpu.VMEM((n, PACK, half), BF),
            pltpu.SemaphoreType.DMA((16,)),
            pltpu.SemaphoreType.DMA((n + 1,)),
        ],
        compiler_params=pltpu.CompilerParams(vmem_limit_bytes=40 * MIB),
        cost_estimate=pl.CostEstimate(flops=2 * rows * width * 6 * hidden, bytes_accessed=28 * MIB, transcendentals=0),
        name="middle",
    )(to, at_row, *gs, xs, wd, wcat, cs, act)


def unpack_kernel(in_ref, gate_ref, up_ref, down_ref):
    per, hidden = gate_ref.shape
    slab = down_ref.shape[0]
    base = 2 * hidden * per // 128
    for q in range(per // 128):
        both = in_ref[q * 2 * hidden : (q + 1) * 2 * hidden, :].T
        gate_ref[q * 128 : (q + 1) * 128, :] = both[:, :hidden]
        up_ref[q * 128 : (q + 1) * 128, :] = both[:, hidden:]
    for q in range(down_ref.shape[1] // 128):
        down_ref[:, q * 128 : (q + 1) * 128] = in_ref[base + q * slab : base + (q + 1) * slab, :]


def unpack(summed, per, hidden, width, slab):
    vmem = pl.BlockSpec(memory_space=pltpu.VMEM)
    return pl.pallas_call(
        unpack_kernel,
        out_shape=(
            jax.ShapeDtypeStruct((per, hidden), BF),
            jax.ShapeDtypeStruct((per, hidden), BF),
            jax.ShapeDtypeStruct((slab, width), BF),
        ),
        in_specs=[vmem],
        out_specs=(vmem, vmem, vmem),
        cost_estimate=pl.CostEstimate(flops=0, bytes_accessed=2 * MIB, transcendentals=0),
        name="unpack",
    )(summed)


def combine_kernel(ids_ref, ret_ref, out_ref, main_ref, rest_ref):
    experts, _, cols = ret_ref.shape
    toks = out_ref.shape[0]
    half = out_ref.shape[1] // 2
    c = pl.program_id(0)

    @pl.when(c == 0)
    def _():
        pos, _, _ = positions(ids_ref[...], experts)
        main, rest = select(pos)
        left = is_left(*rest.shape)
        main_ref[...] = main.T.astype(BF)
        rest_ref[0] = jnp.where(left, rest, 0.0).T.astype(BF)
        rest_ref[1] = jnp.where(left, 0.0, rest).T.astype(BF)

    tail = ret_ref[:, 2 * MAIN : PACK, :].reshape(experts * 2 * REM, cols)
    for side in range(2):
        body = ret_ref[:, side * MAIN : (side + 1) * MAIN, :].reshape(experts * MAIN, cols)
        total = dot(main_ref[...], body) + dot(rest_ref[side], tail)
        out_ref[:, pl.ds(pl.multiple_of(side * half + c * cols, 128), cols)] = total.astype(BF)


def combine(ids, ret):
    experts, _, half = ret.shape
    toks = ids.shape[1]
    steps = 4
    cols = half // steps
    return pl.pallas_call(
        combine_kernel,
        out_shape=jax.ShapeDtypeStruct((toks, 2 * half), BF),
        grid=(steps,),
        in_specs=[
            pl.BlockSpec(ids.shape, lambda c: (0, 0)),
            pl.BlockSpec((experts, PACK, cols), lambda c: (0, 0, c)),
        ],
        out_specs=pl.BlockSpec((toks, 2 * half), lambda c: (0, 0)),
        scratch_shapes=[
            pltpu.VMEM((toks, experts * MAIN), BF),
            pltpu.VMEM((2, toks, experts * 2 * REM), BF),
        ],
        compiler_params=pltpu.CompilerParams(vmem_limit_bytes=24 * MIB),
        cost_estimate=pl.CostEstimate(flops=2 * 1280 * toks * 2 * half, bytes_accessed=6 * MIB, transcendentals=0),
        name="combine",
    )(ids, ret)


def place(x, y, core):
    return (x % SIDE * SIDE + y % SIDE) * CORES + core


def moved(value, dx, dy, flip):
    if dx == dy == flip == 0:
        return value
    pairs = []
    for x in range(SIDE):
        for y in range(SIDE):
            for core in range(CORES):
                pairs.append((place(x, y, core), place(x + dx, y + dy, core ^ flip)))
    return lax.ppermute(value, "expert", pairs)


def shards(tokens, grad_out, gates, expert_ids, w_gate, w_up, w_down):
    copies = lax.axis_size("dp")
    wg, wu, wd = w_gate[0], w_up[0], w_down[0]
    width, hidden = wg.shape
    me = lax.axis_index("expert")
    x, y, core = me // (SIDE * CORES), me // CORES % SIDE, me % CORES
    wide = lambda values: jnp.broadcast_to(jnp.stack(values).astype(jnp.int32)[:, None], (len(values), 128))
    along_y = wide([place(x, d, f) for d, f in SHIFTS])
    along_x = wide([place(x + d, y, core ^ f) for d, f in SPREAD])
    toks = tokens.shape[0]
    near = jnp.arange(SIDE, dtype=jnp.int32)
    starts_x = near * toks
    starts_g = (y - near + SIDE) % SIDE * toks
    origin = jnp.stack([place(x - d + SIDE, b, f) for b, f in SHIFTS for d in range(SIDE)]).astype(jnp.int32)
    at_row = jnp.stack([(d * CORES + (core ^ f)) * SIDE * (MAIN + REM) for d, f in SPREAD]).astype(jnp.int32)

    ids_t = expert_ids.T
    tokens, grad_out = prepare(ids_t, gates.T, tokens, grad_out)
    near_x, near_g = [tokens], [grad_out]
    for d in (1, SIDE - 1):
        near_x.append(moved(tokens, d, 0, 0))
        near_g.append(moved(grad_out, 0, d, 0))
    cut = toks // 2
    lines_x = [tokens, near_x[1], moved(near_x[1][:cut], 1, 0, 0), moved(near_x[2][cut:], SIDE - 1, 0, 0), near_x[2]]
    lines_g = [grad_out, near_g[1], moved(near_g[1][:cut], 0, 1, 0), moved(near_g[2][cut:], 0, SIDE - 1, 0), near_g[2]]
    lines_x, lines_g = lax.optimization_barrier((lines_x, lines_g))
    (out_x,) = dispatch(along_y, starts_x, lines_x, False)
    columns = [[place(a, b, f) for b in range(SIDE) for f in range(CORES)] for a in range(SIDE)]
    xs = lax.all_to_all(out_x, "expert", split_axis=0, concat_axis=0, axis_index_groups=columns, tiled=True)
    along_x, _ = lax.optimization_barrier((along_x, out_x))
    out_g = dispatch(along_x, starts_g, lines_g, True)
    gs = [moved(v, d, 0, f) for v, (d, f) in zip(out_g, SPREAD)]
    cs, act, wcat = forward(xs, wg, wu)
    packed, outgoing = middle(origin, at_row, gs, xs, wd, wcat, cs, act, copies)
    summed = lax.psum_scatter(packed, "dp", scatter_dimension=0, tiled=True)[0]
    ret = lax.all_to_all(outgoing, "expert", split_axis=0, concat_axis=0, tiled=True)
    grad_tokens = combine(ids_t, ret)
    grad_g, grad_u, grad_d = unpack(summed, width // copies, hidden, width, hidden // copies)
    return (grad_tokens, grad_g[None], grad_u[None], grad_d[None])


def solution(mesh):
    rows = P(("dp", "expert"), None)
    weights = P("expert", None, None)
    cut = P("expert", "dp", None)
    return jax.shard_map(
        shards,
        mesh=mesh,
        in_specs=(rows, rows, rows, rows, weights, weights, weights),
        out_specs=(rows, cut, cut, cut),
        check_vma=False,
    )
```

```python
import functools

import jax
import jax.numpy as jnp
from jax import lax
from jax.experimental import pallas as pl
from jax.experimental.pallas import tpu as pltpu
from jax.sharding import PartitionSpec as P

BF = jnp.bfloat16
F32 = jnp.float32
MIB = 1 << 20

MAIN = 32
REM = 4
PACK = 2 * (MAIN + REM)


SIDE = 4
CORES = 2
SHIFTS = [(d, f) for d in range(SIDE) for f in range(CORES)]
SPREAD = [(0, 0), (1, 0), (3, 0), (2, 0), (1, 1), (3, 1), (2, 1), (0, 1)]


def dot(a, b, ca=1, cb=0):
    return lax.dot_general(a, b, (((ca,), (cb,)), ((), ())), preferred_element_type=F32)


def iota(shape, dim):
    return lax.broadcasted_iota(jnp.int32, shape, dim)


def positions(ids, experts):
    top, toks = ids.shape
    ids_t = ids.astype(F32)
    ident = iota((experts, toks), 0).astype(F32)
    member = jnp.zeros((experts, toks), F32)
    for k in range(top):
        member = member + jnp.where(ids_t[k : k + 1, :] == ident, 1.0, 0.0)
    before = (iota((toks, toks), 0) < iota((toks, toks), 1)).astype(F32).astype(BF)
    pos = dot(member.astype(BF), before)
    return jnp.where(member > 0.5, pos, -1.0), ids_t, ident


def select(pos):
    experts, toks = pos.shape
    wide = pos[:, None, :]
    main = (wide == iota((experts, MAIN, toks), 1).astype(F32)).astype(F32)
    rest = (wide == (MAIN + iota((experts, 2 * REM, toks), 1) % REM).astype(F32)).astype(F32)
    return main.reshape(experts * MAIN, toks), rest.reshape(experts * 2 * REM, toks)


def is_left(rows, cols):
    return iota((rows, cols), 0) % (2 * REM) < REM


def prepare_kernel(ids_hbm, gates_hbm, tokens_hbm, grads_hbm, tokens_out, grads_out, row_ref, ids_ref, gates_ref, sems):
    width = tokens_hbm.shape[1]
    loads = [
        pltpu.make_async_copy(src, row_ref.at[n, :, :width], sems.at[n]) for n, src in enumerate((tokens_hbm, grads_hbm))
    ]
    small = [pltpu.make_async_copy(ids_hbm, ids_ref, sems.at[4]), pltpu.make_async_copy(gates_hbm, gates_ref, sems.at[5])]
    for load in small + loads:
        load.start()
    for load in small:
        load.wait()
    pos, ids_t, ident = positions(ids_ref[...], 32)
    gates_t = gates_ref[...]
    weight = jnp.zeros(pos.shape, F32)
    for k in range(gates_t.shape[0]):
        weight = weight + jnp.where(ids_t[k : k + 1, :] == ident, gates_t[k : k + 1, :], 0.0)
    high = weight.astype(BF).astype(F32)
    mid = (weight - high).astype(BF).astype(F32)
    low = weight - high - mid
    extra = jnp.concatenate([pos, high, mid, low], axis=0).T.astype(BF)
    stores = []
    for n, dst in enumerate((tokens_out, grads_out)):
        row_ref[n, :, width:] = extra
        loads[n].wait()
        stores.append(pltpu.make_async_copy(row_ref.at[n], dst, sems.at[2 + n]))
        stores[-1].start()
    for store in stores:
        store.wait()


HBM = pl.BlockSpec(memory_space=pltpu.HBM)
VMEM = pl.BlockSpec(memory_space=pltpu.VMEM)


def in_hbm(*arrays):
    return [pltpu.with_memory_space_constraint(a, pltpu.HBM) for a in arrays]


def prepare(ids, gates, tokens, grads):
    toks, width = tokens.shape
    shape = pltpu.HBM((toks, width + 128), BF)
    return pl.pallas_call(
        prepare_kernel,
        out_shape=(shape, shape),
        in_specs=[HBM] * 4,
        out_specs=(HBM, HBM),
        scratch_shapes=[
            pltpu.VMEM((2, toks, width + 128), BF),
            pltpu.VMEM(ids.shape, ids.dtype),
            pltpu.VMEM(gates.shape, F32),
            pltpu.SemaphoreType.DMA((6,)),
        ],
        compiler_params=pltpu.CompilerParams(vmem_limit_bytes=16 * MIB),
        cost_estimate=pl.CostEstimate(flops=1 << 20, bytes_accessed=2 * MIB, transcendentals=0),
        name="prepare",
    )(*in_hbm(ids, gates, tokens, grads))


def dispatch_kernel(scaled, per, wanted_ref, starts_ref, *refs):
    lines, pieces = 4, 5
    sources = refs[:pieces]
    count = 8 if scaled else 1
    outs = refs[pieces : pieces + count]
    data_ref, extra_ref, s_ref, out_ref, scale_ref, in_sems, out_sems = refs[pieces + count :]
    experts, rows, width = out_ref.shape
    toks = sources[0].shape[0]

    loads = []
    for k, (src, line, above) in enumerate(zip(sources, (0, 1, 2, 2, 3), (0, 0, 0, toks // 2, 0))):
        row = pl.multiple_of(starts_ref[line] + above, 16)
        some = pl.ds(row, src.shape[0])
        loads.append(pltpu.make_async_copy(src.at[:, width:], extra_ref.at[some, :], in_sems.at[k]))
        loads.append(pltpu.make_async_copy(src.at[:, :width], data_ref.at[some, :], in_sems.at[pieces + k]))
    for load in loads[0::2] + loads[1::2]:
        load.start()
    for load in loads[0::2]:
        load.wait()

    extra = extra_ref[...]
    wanted = wanted_ref[...]
    lane = iota(wanted.shape, 1)

    def column(piece):
        pick = (lane == wanted + piece * 32).astype(F32).astype(BF)
        return dot(pick, extra, 1, 1)

    pos = column(0)
    pair, some = rows // 2, lines * toks // 2
    for h in range(2):
        mine = slice(h * some, (h + 1) * some)
        first = (iota((experts, some), 1) // toks * per).astype(F32)
        target = jnp.where(pos[:, mine] >= 0.0, pos[:, mine] + first, -1.0)
        chosen = target[:, None, :] == iota((experts, pair, some), 1).astype(F32)
        chosen = chosen.astype(F32)
        s_ref[h] = chosen.reshape(experts * pair, some).astype(BF)
        if scaled:
            weight = (column(1) + (column(2) + column(3)))[:, mine]
            total = jnp.sum(chosen * weight[:, None, :], axis=2, keepdims=True)
            scale_ref[h] = jnp.broadcast_to(total, (experts, pair, 128)).reshape(experts * pair, 128)

    for load in loads[1::2]:
        load.wait()
    stores = []
    parts = 4
    columns = width // parts
    for c in range(parts):
        cols = slice(c * columns, (c + 1) * columns)
        for h in range(2):
            got = dot(s_ref[h], data_ref[h * some : (h + 1) * some, cols])
            if scaled:
                got = got * jnp.concatenate([scale_ref[h]] * (columns // 128), axis=1)
            out_ref[:, h * pair : (h + 1) * pair, cols] = got.astype(BF).reshape(experts, pair, columns)
        for k, out in enumerate(outs):
            here, there = (out_ref.at[k], out) if scaled else (out_ref, out)
            at = (slice(None),) * (len(there.shape) - 1) + (cols,)
            stores.append(pltpu.make_async_copy(here.at[at], there.at[at], out_sems.at[c * count + k]))
            stores[-1].start()
    for store in stores:
        store.wait()


def dispatch(wanted, starts, lines, scaled):
    toks, width = lines[0].shape[0], lines[0].shape[1] - 128
    per, experts = MAIN + REM, 8
    rows, all_toks = SIDE * per, SIDE * toks
    shapes = (pltpu.HBM((rows, width), BF),) * experts if scaled else (pltpu.HBM((experts, rows, width), BF),)
    return pl.pallas_call(
        functools.partial(dispatch_kernel, scaled, per),
        out_shape=shapes,
        in_specs=[VMEM, pl.BlockSpec(memory_space=pltpu.SMEM)] + [HBM] * len(lines),
        out_specs=(HBM,) * len(shapes),
        scratch_shapes=[
            pltpu.VMEM((all_toks, width), BF),
            pltpu.VMEM((all_toks, 128), BF),
            pltpu.VMEM((2, experts * rows // 2, all_toks // 2), BF),
            pltpu.VMEM((experts, rows, width), BF),
            pltpu.VMEM((2, experts * rows // 2, 128), F32),
            pltpu.SemaphoreType.DMA((2 * len(lines),)),
            pltpu.SemaphoreType.DMA((4 * len(shapes),)),
        ],
        compiler_params=pltpu.CompilerParams(vmem_limit_bytes=32 * MIB),
        cost_estimate=pl.CostEstimate(
            flops=2 * experts * rows * all_toks * width, bytes_accessed=7 * MIB, transcendentals=0
        ),
        name="dispatch",
    )(wanted, starts, *in_hbm(*lines))


def regrouped(block):
    return block % 4 * 8 + block // 4 % 2 * 4 + block // 8


def forward_kernel(*refs):
    blocks, wg_hbm, wu_hbm = refs[:3]
    cs_ref, at_ref, wcat_ref, x_ref = refs[3:7]
    act_ref, turn_ref, sems = refs[7:]
    rows = blocks.shape[1]
    hidden = wg_hbm.shape[1]
    loads = [
        pltpu.make_async_copy(wg_hbm, wcat_ref.at[:, :hidden], sems.at[8]),
        pltpu.make_async_copy(wu_hbm, wcat_ref.at[:, hidden:], sems.at[9]),
    ]
    loads += [
        pltpu.make_async_copy(blocks.at[k], x_ref.at[k * rows : (k + 1) * rows, :], sems.at[k]) for k in range(8)
    ]
    for load in loads:
        load.start()
    loads[0].wait()
    loads[1].wait()
    parts = 4
    most = 8 // parts * rows
    for i in range(parts):
        for load in loads[2 + i * 8 // parts : 2 + (i + 1) * 8 // parts]:
            load.wait()
        some = slice(i * most, (i + 1) * most)
        pre = dot(x_ref[some, :], wcat_ref[...])
        gate, up = pre[:, :hidden], pre[:, hidden:]
        sigma = jax.nn.sigmoid(gate)
        silu = gate * sigma
        cs_ref[some, :hidden] = up * sigma * (1.0 + gate * (1.0 - sigma))
        cs_ref[some, hidden:] = silu
        act_ref[some, :] = silu * up
    per = MAIN + REM
    for b in range(32):
        to = regrouped(b)
        turn_ref[to * per : (to + 1) * per, :] = act_ref[b * per : (b + 1) * per, :]
    at_ref[...] = turn_ref[...].astype(BF).T


def forward(blocks, wg, wu):
    width, hidden = wg.shape
    rows = 8 * blocks.shape[1]
    return pl.pallas_call(
        forward_kernel,
        out_shape=(
            jax.ShapeDtypeStruct((rows, 2 * hidden), F32),
            jax.ShapeDtypeStruct((hidden, rows), BF),
            jax.ShapeDtypeStruct((width, 2 * hidden), BF),
            jax.ShapeDtypeStruct((rows, width), BF),
        ),
        in_specs=[HBM] * 3,
        out_specs=(VMEM,) * 4,
        scratch_shapes=[
            pltpu.VMEM((rows, hidden), F32),
            pltpu.VMEM((rows, hidden), F32),
            pltpu.SemaphoreType.DMA((10,)),
        ],
        compiler_params=pltpu.CompilerParams(vmem_limit_bytes=20 * MIB),
        cost_estimate=pl.CostEstimate(
            flops=2 * rows * width * 2 * hidden, bytes_accessed=16 * MIB, transcendentals=rows * hidden
        ),
        name="forward",
    )(*in_hbm(blocks, wg, wu))


def middle_kernel(*refs):
    to_ref, at_row_ref, gs, x_ref = refs[0], refs[1], refs[2:10], refs[10]
    wd_ref, wcat_ref, cs_ref, at_ref = refs[11:15]
    packed_hbm, pair_hbm = refs[15:17]
    (g_ref, raw_ref, turn_ref, d_ref, dt_ref, dm_ref, dr_ref, packed_ref,
     pair_ref, sems, out_sems) = refs[17:]
    rows = gs[0].shape[0]
    copies = packed_ref.shape[0]
    n, _, half = pair_ref.shape
    hidden, both = at_ref.shape[0], wcat_ref.shape[1]
    per_block = MAIN + REM

    def load(src, dst, sem):
        copy = pltpu.make_async_copy(src, dst, sems.at[sem])
        copy.start()
        return copy

    order = sorted(range(8), key=lambda k: SPREAD[k])
    g_in = [load(gs[k], g_ref.at[pl.ds(pl.multiple_of(at_row_ref[k], 16), rows), :], k) for k in order]

    parts = 2
    most = 8 // parts * rows
    for i in range(parts):
        for copy in g_in[i * 8 // parts : (i + 1) * 8 // parts]:
            copy.wait()
        some = slice(i * most, (i + 1) * most)
        raw_ref[some, :] = dot(g_ref[some, :], wd_ref[...], 1, 1)
    for b in range(n):
        to = regrouped(b)
        turn_ref[to * per_block : (to + 1) * per_block, :] = raw_ref[b * per_block : (b + 1) * per_block, :]
    for i in range(parts):
        some = slice(i * most, (i + 1) * most)
        d_act = turn_ref[some, :]
        grad = jnp.concatenate([d_act, d_act], axis=1) * cs_ref[some, :]
        d_ref[some, :] = grad
    dr_ref[...] = jnp.zeros_like(dr_ref)
    for b in range(n):
        dm_ref[b * MAIN : (b + 1) * MAIN, :] = d_ref[b * per_block : b * per_block + MAIN, :].astype(BF)
        dr_ref[b * 2 * REM : b * 2 * REM + REM, :] = d_ref[b * per_block + MAIN : (b + 1) * per_block, :]

    tile = 256
    per = 2 * half // copies
    slab = hidden // copies
    base = both * per // 128
    tiles = 2 * half // tile
    turns = 8 * rows // 128
    for j in range(max(tiles, turns)):
        if j < turns:
            some = slice(j * 128, (j + 1) * 128)
            dt_ref[:, some] = d_ref[some, :].astype(BF).T
        if j < tiles:
            down = dot(at_ref[...], g_ref[:, j * tile : (j + 1) * tile]).astype(BF)
            for q in range(tile // 128):
                at = j * tile // 128 + q
                part = down[:, q * 128 : (q + 1) * 128].reshape(copies, slab, 128)
                packed_ref[:, base + at * slab : base + (at + 1) * slab, :] = part
    for j in range(tiles):
        into = dot(dt_ref[...], x_ref[:, j * tile : (j + 1) * tile]).astype(BF)
        for q in range(tile // 128):
            at = j * tile // 128 + q
            owner, piece = at * 128 // per, at % (per // 128)
            packed_ref[owner, piece * both : (piece + 1) * both, :] = into[:, q * 128 : (q + 1) * 128]
    packed_out = pltpu.make_async_copy(packed_ref, packed_hbm, out_sems.at[n])
    packed_out.start()

    sent = []
    parts = 4
    step = n // parts
    most, few = step * MAIN, step * 2 * REM
    for i in range(parts):
        main = dm_ref[i * most : (i + 1) * most, :]
        rest = dr_ref[i * few : (i + 1) * few, :]
        d_left = jnp.concatenate([main, rest.astype(BF)], axis=0)
        d_right = jnp.concatenate([main, pltpu.roll(rest, REM, 0).astype(BF)], axis=0)
        y_left = dot(d_left, wcat_ref[:half, :], 1, 1)
        y_right = dot(d_right, wcat_ref[half:, :], 1, 1)
        some = slice(i * step, (i + 1) * step)
        pair_ref[some, 0:MAIN, :] = y_left[:most].astype(BF).reshape(step, MAIN, half)
        pair_ref[some, MAIN : 2 * MAIN, :] = y_right[:most].astype(BF).reshape(step, MAIN, half)
        tail = (y_left[most:] + y_right[most:]).astype(BF)
        pair_ref[some, 2 * MAIN : PACK, :] = tail.reshape(step, 2 * REM, half)
        for b in range(i * step, (i + 1) * step):
            copy = pltpu.make_async_copy(pair_ref.at[b], pair_hbm.at[to_ref[b]], out_sems.at[b])
            copy.start()
            sent.append(copy)
    for copy in sent:
        copy.wait()
    packed_out.wait()


def middle(to, at_row, gs, xs, wd, wcat, cs, act, copies):
    hidden, width = wd.shape
    both, rows = cs.shape[1], cs.shape[0]
    n, half = to.shape[0], width // 2
    length = 3 * hidden * width // copies // 128
    smem = pl.BlockSpec(memory_space=pltpu.SMEM)
    return pl.pallas_call(
        middle_kernel,
        out_shape=(pltpu.HBM((copies, length, 128), BF), pltpu.HBM((n, PACK, half), BF)),
        in_specs=[smem] * 2 + [pl.BlockSpec(memory_space=pl.ANY)] * 8 + [VMEM] * 5,
        out_specs=(HBM,) * 2,
        scratch_shapes=[
            pltpu.VMEM((rows, width), BF),
            pltpu.VMEM((rows, hidden), F32),
            pltpu.VMEM((rows, hidden), F32),
            pltpu.VMEM((rows, both), F32),
            pltpu.VMEM((both, rows), BF),
            pltpu.VMEM((n * MAIN, both), BF),
            pltpu.VMEM((n * 2 * REM, both), F32),
            pltpu.VMEM((copies, length, 128), BF),
            pltpu.VMEM((n, PACK, half), BF),
            pltpu.SemaphoreType.DMA((8,)),
            pltpu.SemaphoreType.DMA((n + 1,)),
        ],
        compiler_params=pltpu.CompilerParams(vmem_limit_bytes=36 * MIB),
        cost_estimate=pl.CostEstimate(flops=2 * rows * width * 6 * hidden, bytes_accessed=28 * MIB, transcendentals=0),
        name="middle",
    )(to, at_row, *gs, xs, wd, wcat, cs, act)


def unpack_kernel(in_ref, gate_ref, up_ref, down_ref):
    per, hidden = gate_ref.shape
    slab = down_ref.shape[0]
    base = 2 * hidden * per // 128
    for q in range(per // 128):
        both = in_ref[q * 2 * hidden : (q + 1) * 2 * hidden, :].T
        gate_ref[q * 128 : (q + 1) * 128, :] = both[:, :hidden]
        up_ref[q * 128 : (q + 1) * 128, :] = both[:, hidden:]
    for q in range(down_ref.shape[1] // 128):
        down_ref[:, q * 128 : (q + 1) * 128] = in_ref[base + q * slab : base + (q + 1) * slab, :]


def combine_kernel(ids_ref, ret_ref, sum_ref, out_ref, gate_ref, up_ref, down_ref, main_ref, rest_ref):
    experts, _, cols = ret_ref.shape
    toks = out_ref.shape[0]
    half = out_ref.shape[1] // 2
    c = pl.program_id(0)

    @pl.when(c == 0)
    def _():
        pos, _, _ = positions(ids_ref[...], experts)
        main, rest = select(pos)
        left = is_left(*rest.shape)
        main_ref[...] = main.T.astype(BF)
        rest_ref[0] = jnp.where(left, rest, 0.0).T.astype(BF)
        rest_ref[1] = jnp.where(left, 0.0, rest).T.astype(BF)

    @pl.when(c == 1)
    def _():
        unpack_kernel(sum_ref, gate_ref, up_ref, down_ref)

    tail = ret_ref[:, 2 * MAIN : PACK, :].reshape(experts * 2 * REM, cols)
    for side in range(2):
        body = ret_ref[:, side * MAIN : (side + 1) * MAIN, :].reshape(experts * MAIN, cols)
        total = dot(main_ref[...], body) + dot(rest_ref[side], tail)
        out_ref[:, pl.ds(pl.multiple_of(side * half + c * cols, 128), cols)] = total.astype(BF)


def combine(ids, ret, summed, per, hidden, slab):
    experts, _, half = ret.shape
    toks = ids.shape[1]
    steps = 4
    cols = half // steps
    shapes = ((toks, 2 * half), (per, hidden), (per, hidden), (slab, 2 * half))
    return pl.pallas_call(
        combine_kernel,
        out_shape=tuple(jax.ShapeDtypeStruct(shape, BF) for shape in shapes),
        grid=(steps,),
        in_specs=[
            pl.BlockSpec(ids.shape, lambda c: (0, 0)),
            pl.BlockSpec((experts, PACK, cols), lambda c: (0, 0, c)),
            pl.BlockSpec(summed.shape, lambda c: (0, 0)),
        ],
        out_specs=tuple(pl.BlockSpec(shape, lambda c: (0, 0)) for shape in shapes),
        scratch_shapes=[
            pltpu.VMEM((toks, experts * MAIN), BF),
            pltpu.VMEM((2, toks, experts * 2 * REM), BF),
        ],
        compiler_params=pltpu.CompilerParams(vmem_limit_bytes=24 * MIB),
        cost_estimate=pl.CostEstimate(flops=2 * 1280 * toks * 2 * half, bytes_accessed=6 * MIB, transcendentals=0),
        name="combine",
    )(ids, ret, summed)


def place(x, y, core):
    return (x % SIDE * SIDE + y % SIDE) * CORES + core


def moved(value, dx, dy, flip):
    if dx == dy == flip == 0:
        return value
    pairs = []
    for x in range(SIDE):
        for y in range(SIDE):
            for core in range(CORES):
                pairs.append((place(x, y, core), place(x + dx, y + dy, core ^ flip)))
    return lax.ppermute(value, "expert", pairs)


def shards(tokens, grad_out, gates, expert_ids, w_gate, w_up, w_down):
    copies = lax.axis_size("dp")
    wg, wu, wd = w_gate[0], w_up[0], w_down[0]
    width, hidden = wg.shape
    me = lax.axis_index("expert")
    x, y, core = me // (SIDE * CORES), me // CORES % SIDE, me % CORES
    wide = lambda values: jnp.broadcast_to(jnp.stack(values).astype(jnp.int32)[:, None], (len(values), 128))
    along_y = wide([place(x, d, f) for d, f in SHIFTS])
    along_x = wide([place(x + d, y, core ^ f) for d, f in SPREAD])
    toks = tokens.shape[0]
    near = jnp.arange(SIDE, dtype=jnp.int32)
    starts_x = near * toks
    starts_g = (y - near + SIDE) % SIDE * toks
    origin = jnp.stack([place(x - d + SIDE, b, f) for b, f in SHIFTS for d in range(SIDE)]).astype(jnp.int32)
    at_row = jnp.stack([(d * CORES + (core ^ f)) * SIDE * (MAIN + REM) for d, f in SPREAD]).astype(jnp.int32)

    ids_t = expert_ids.T
    tokens, grad_out = prepare(ids_t, gates.T, tokens, grad_out)
    near_x, near_g = [tokens], [grad_out]
    for d in (1, SIDE - 1):
        near_x.append(moved(tokens, d, 0, 0))
        near_g.append(moved(grad_out, 0, d, 0))
    cut = toks // 2
    lines_x = [tokens, near_x[1], moved(near_x[1][:cut], 1, 0, 0), moved(near_x[2][cut:], SIDE - 1, 0, 0), near_x[2]]
    lines_g = [grad_out, near_g[1], moved(near_g[1][:cut], 0, 1, 0), moved(near_g[2][cut:], 0, SIDE - 1, 0), near_g[2]]
    lines_x, lines_g = lax.optimization_barrier((lines_x, lines_g))
    (out_x,) = dispatch(along_y, starts_x, lines_x, False)
    columns = [[place(a, b, f) for b in range(SIDE) for f in range(CORES)] for a in range(SIDE)]
    xs = lax.all_to_all(out_x, "expert", split_axis=0, concat_axis=0, axis_index_groups=columns, tiled=True)
    along_x, _ = lax.optimization_barrier((along_x, out_x))
    out_g = dispatch(along_x, starts_g, lines_g, True)
    gs = [moved(v, d, 0, f) for v, (d, f) in zip(out_g, SPREAD)]
    cs, act, wcat, rows_x = forward(xs, wg, wu)
    packed, outgoing = middle(origin, at_row, gs, rows_x, wd, wcat, cs, act, copies)
    summed = lax.psum_scatter(packed, "dp", scatter_dimension=0, tiled=True)[0]
    ret = lax.all_to_all(outgoing, "expert", split_axis=0, concat_axis=0, tiled=True)
    grad_tokens, grad_g, grad_u, grad_d = combine(ids_t, ret, summed, width // copies, hidden, hidden // copies)
    return (grad_tokens, grad_g[None], grad_u[None], grad_d[None])


def solution(mesh):
    rows = P(("dp", "expert"), None)
    weights = P("expert", None, None)
    cut = P("expert", "dp", None)
    return jax.shard_map(
        shards,
        mesh=mesh,
        in_specs=(rows, rows, rows, rows, weights, weights, weights),
        out_specs=(rows, cut, cut, cut),
        check_vma=False,
    )
```

```python
import functools

import jax
import jax.numpy as jnp
from jax import lax
from jax.experimental import pallas as pl
from jax.experimental.pallas import tpu as pltpu
from jax.sharding import PartitionSpec as P

BF = jnp.bfloat16
F32 = jnp.float32
MIB = 1 << 20

MAIN = 32
REM = 4
PACK = 2 * (MAIN + REM)


SIDE = 4
CORES = 2
SHIFTS = [(d, f) for d in range(SIDE) for f in range(CORES)]
SPREAD = [(0, 0), (1, 0), (3, 0), (2, 0), (1, 1), (3, 1), (2, 1), (0, 1)]


def dot(a, b, ca=1, cb=0):
    return lax.dot_general(a, b, (((ca,), (cb,)), ((), ())), preferred_element_type=F32)


def iota(shape, dim):
    return lax.broadcasted_iota(jnp.int32, shape, dim)


def positions(ids, experts):
    top, toks = ids.shape
    ids_t = ids.astype(F32)
    ident = iota((experts, toks), 0).astype(F32)
    member = jnp.zeros((experts, toks), F32)
    for k in range(top):
        member = member + jnp.where(ids_t[k : k + 1, :] == ident, 1.0, 0.0)
    before = (iota((toks, toks), 0) < iota((toks, toks), 1)).astype(F32).astype(BF)
    pos = dot(member.astype(BF), before)
    return jnp.where(member > 0.5, pos, -1.0), ids_t, ident


def select(pos):
    experts, toks = pos.shape
    wide = pos[:, None, :]
    main = (wide == iota((experts, MAIN, toks), 1).astype(F32)).astype(F32)
    rest = (wide == (MAIN + iota((experts, 2 * REM, toks), 1) % REM).astype(F32)).astype(F32)
    return main.reshape(experts * MAIN, toks), rest.reshape(experts * 2 * REM, toks)


def is_left(rows, cols):
    return iota((rows, cols), 0) % (2 * REM) < REM


def prepare_kernel(ids_hbm, gates_hbm, tokens_hbm, grads_hbm, tokens_out, grads_out, row_ref, ids_ref, gates_ref, sems):
    width = tokens_hbm.shape[1]
    loads = [
        pltpu.make_async_copy(src, row_ref.at[n, :, :width], sems.at[n]) for n, src in enumerate((tokens_hbm, grads_hbm))
    ]
    small = [pltpu.make_async_copy(ids_hbm, ids_ref, sems.at[4]), pltpu.make_async_copy(gates_hbm, gates_ref, sems.at[5])]
    for load in small + loads:
        load.start()
    for load in small:
        load.wait()
    pos, ids_t, ident = positions(ids_ref[...], 32)
    gates_t = gates_ref[...]
    weight = jnp.zeros(pos.shape, F32)
    for k in range(gates_t.shape[0]):
        weight = weight + jnp.where(ids_t[k : k + 1, :] == ident, gates_t[k : k + 1, :], 0.0)
    high = weight.astype(BF).astype(F32)
    mid = (weight - high).astype(BF).astype(F32)
    low = weight - high - mid
    extra = jnp.concatenate([pos, high, mid, low], axis=0).T.astype(BF)
    stores = []
    for n, dst in enumerate((tokens_out, grads_out)):
        row_ref[n, :, width:] = extra
        loads[n].wait()
        stores.append(pltpu.make_async_copy(row_ref.at[n], dst, sems.at[2 + n]))
        stores[-1].start()
    for store in stores:
        store.wait()


HBM = pl.BlockSpec(memory_space=pltpu.HBM)
VMEM = pl.BlockSpec(memory_space=pltpu.VMEM)


def in_hbm(*arrays):
    return [pltpu.with_memory_space_constraint(a, pltpu.HBM) for a in arrays]


def prepare(ids, gates, tokens, grads):
    toks, width = tokens.shape
    shape = pltpu.HBM((toks, width + 128), BF)
    return pl.pallas_call(
        prepare_kernel,
        out_shape=(shape, shape),
        in_specs=[HBM] * 4,
        out_specs=(HBM, HBM),
        scratch_shapes=[
            pltpu.VMEM((2, toks, width + 128), BF),
            pltpu.VMEM(ids.shape, ids.dtype),
            pltpu.VMEM(gates.shape, F32),
            pltpu.SemaphoreType.DMA((6,)),
        ],
        compiler_params=pltpu.CompilerParams(vmem_limit_bytes=16 * MIB),
        cost_estimate=pl.CostEstimate(flops=1 << 20, bytes_accessed=2 * MIB, transcendentals=0),
        name="prepare",
    )(*in_hbm(ids, gates, tokens, grads))


def dispatch_kernel(scaled, per, wanted_ref, starts_ref, *refs):
    lines, pieces = 4, 5
    sources = refs[:pieces]
    count = 8 if scaled else 1
    outs = refs[pieces : pieces + count]
    data_ref, extra_ref, s_ref, out_ref, scale_ref, in_sems, out_sems = refs[pieces + count :]
    experts, rows, width = out_ref.shape
    toks = sources[0].shape[0]

    loads = []
    for k, (src, line, above) in enumerate(zip(sources, (0, 1, 2, 2, 3), (0, 0, 0, toks // 2, 0))):
        row = pl.multiple_of(starts_ref[line] + above, 16)
        some = pl.ds(row, src.shape[0])
        loads.append(pltpu.make_async_copy(src.at[:, width:], extra_ref.at[some, :], in_sems.at[k]))
        loads.append(pltpu.make_async_copy(src.at[:, :width], data_ref.at[some, :], in_sems.at[pieces + k]))
    for load in loads[0::2] + loads[1::2]:
        load.start()
    for load in loads[0::2]:
        load.wait()

    extra = extra_ref[...]
    wanted = wanted_ref[...]
    lane = iota(wanted.shape, 1)

    def column(piece):
        pick = (lane == wanted + piece * 32).astype(F32).astype(BF)
        return dot(pick, extra, 1, 1)

    pos = column(0)
    pair, some = rows // 2, lines * toks // 2
    for h in range(2):
        mine = slice(h * some, (h + 1) * some)
        first = (iota((experts, some), 1) // toks * per).astype(F32)
        target = jnp.where(pos[:, mine] >= 0.0, pos[:, mine] + first, -1.0)
        chosen = target[:, None, :] == iota((experts, pair, some), 1).astype(F32)
        chosen = chosen.astype(F32)
        s_ref[h] = chosen.reshape(experts * pair, some).astype(BF)
        if scaled:
            weight = (column(1) + (column(2) + column(3)))[:, mine]
            total = jnp.sum(chosen * weight[:, None, :], axis=2, keepdims=True)
            scale_ref[h] = jnp.broadcast_to(total, (experts, pair, 128)).reshape(experts * pair, 128)

    for load in loads[1::2]:
        load.wait()
    stores = []
    parts = 4
    columns = width // parts
    for c in range(parts):
        cols = slice(c * columns, (c + 1) * columns)
        for h in range(2):
            got = dot(s_ref[h], data_ref[h * some : (h + 1) * some, cols])
            if scaled:
                got = got * jnp.concatenate([scale_ref[h]] * (columns // 128), axis=1)
            out_ref[:, h * pair : (h + 1) * pair, cols] = got.astype(BF).reshape(experts, pair, columns)
        for k, out in enumerate(outs):
            here, there = (out_ref.at[k], out) if scaled else (out_ref, out)
            at = (slice(None),) * (len(there.shape) - 1) + (cols,)
            stores.append(pltpu.make_async_copy(here.at[at], there.at[at], out_sems.at[c * count + k]))
            stores[-1].start()
    for store in stores:
        store.wait()


def dispatch(wanted, starts, lines, scaled):
    toks, width = lines[0].shape[0], lines[0].shape[1] - 128
    per, experts = MAIN + REM, 8
    rows, all_toks = SIDE * per, SIDE * toks
    shapes = (pltpu.HBM((rows, width), BF),) * experts if scaled else (pltpu.HBM((experts, rows, width), BF),)
    return pl.pallas_call(
        functools.partial(dispatch_kernel, scaled, per),
        out_shape=shapes,
        in_specs=[VMEM, pl.BlockSpec(memory_space=pltpu.SMEM)] + [HBM] * len(lines),
        out_specs=(HBM,) * len(shapes),
        scratch_shapes=[
            pltpu.VMEM((all_toks, width), BF),
            pltpu.VMEM((all_toks, 128), BF),
            pltpu.VMEM((2, experts * rows // 2, all_toks // 2), BF),
            pltpu.VMEM((experts, rows, width), BF),
            pltpu.VMEM((2, experts * rows // 2, 128), F32),
            pltpu.SemaphoreType.DMA((2 * len(lines),)),
            pltpu.SemaphoreType.DMA((4 * len(shapes),)),
        ],
        compiler_params=pltpu.CompilerParams(vmem_limit_bytes=32 * MIB),
        cost_estimate=pl.CostEstimate(
            flops=2 * experts * rows * all_toks * width, bytes_accessed=7 * MIB, transcendentals=0
        ),
        name="dispatch",
    )(wanted, starts, *in_hbm(*lines))


def regrouped(block):
    return block % 4 * 8 + block // 4 % 2 * 4 + block // 8


def forward_kernel(*refs):
    blocks, wg_hbm, wu_hbm = refs[:3]
    cs_ref, at_ref, wcat_ref, x_ref = refs[3:7]
    act_ref, turn_ref, sems = refs[7:]
    rows = blocks.shape[1]
    hidden = wg_hbm.shape[1]
    loads = [
        pltpu.make_async_copy(wg_hbm, wcat_ref.at[:, :hidden], sems.at[8]),
        pltpu.make_async_copy(wu_hbm, wcat_ref.at[:, hidden:], sems.at[9]),
    ]
    loads += [
        pltpu.make_async_copy(blocks.at[k], x_ref.at[k * rows : (k + 1) * rows, :], sems.at[k]) for k in range(8)
    ]
    for load in loads:
        load.start()
    loads[0].wait()
    loads[1].wait()
    parts = 4
    most = 8 // parts * rows
    for i in range(parts):
        for load in loads[2 + i * 8 // parts : 2 + (i + 1) * 8 // parts]:
            load.wait()
        some = slice(i * most, (i + 1) * most)
        pre = dot(x_ref[some, :], wcat_ref[...])
        gate, up = pre[:, :hidden], pre[:, hidden:]
        sigma = jax.nn.sigmoid(gate)
        silu = gate * sigma
        cs_ref[some, :hidden] = up * sigma * (1.0 + gate * (1.0 - sigma))
        cs_ref[some, hidden:] = silu
        act_ref[some, :] = silu * up
    per = MAIN + REM
    for b in range(32):
        to = regrouped(b)
        turn_ref[to * per : (to + 1) * per, :] = act_ref[b * per : (b + 1) * per, :]
    at_ref[...] = turn_ref[...].astype(BF).T


def forward(blocks, wg, wu):
    width, hidden = wg.shape
    rows = 8 * blocks.shape[1]
    return pl.pallas_call(
        forward_kernel,
        out_shape=(
            jax.ShapeDtypeStruct((rows, 2 * hidden), F32),
            jax.ShapeDtypeStruct((hidden, rows), BF),
            jax.ShapeDtypeStruct((width, 2 * hidden), BF),
            jax.ShapeDtypeStruct((rows, width), BF),
        ),
        in_specs=[HBM] * 3,
        out_specs=(VMEM,) * 4,
        scratch_shapes=[
            pltpu.VMEM((rows, hidden), F32),
            pltpu.VMEM((rows, hidden), F32),
            pltpu.SemaphoreType.DMA((10,)),
        ],
        compiler_params=pltpu.CompilerParams(vmem_limit_bytes=20 * MIB),
        cost_estimate=pl.CostEstimate(
            flops=2 * rows * width * 2 * hidden, bytes_accessed=16 * MIB, transcendentals=rows * hidden
        ),
        name="forward",
    )(*in_hbm(blocks, wg, wu))


def middle_kernel(*refs):
    to_ref, at_row_ref, gs, x_ref = refs[0], refs[1], refs[2:10], refs[10]
    wd_ref, wcat_ref, cs_ref, at_ref = refs[11:15]
    packed_hbm, pair_hbm = refs[15:17]
    (g_ref, raw_ref, turn_ref, d_ref, dt_ref, dm_ref, dr_ref, packed_ref,
     pair_ref, sems, out_sems) = refs[17:]
    rows = gs[0].shape[0]
    copies = packed_ref.shape[0]
    n, _, half = pair_ref.shape
    hidden, both = at_ref.shape[0], wcat_ref.shape[1]
    per_block = MAIN + REM

    def load(src, dst, sem):
        copy = pltpu.make_async_copy(src, dst, sems.at[sem])
        copy.start()
        return copy

    order = sorted(range(8), key=lambda k: SPREAD[k])
    g_in = [load(gs[k], g_ref.at[pl.ds(pl.multiple_of(at_row_ref[k], 16), rows), :], k) for k in order]

    parts = 2
    most = 8 // parts * rows
    for i in range(parts):
        for copy in g_in[i * 8 // parts : (i + 1) * 8 // parts]:
            copy.wait()
        some = slice(i * most, (i + 1) * most)
        raw_ref[some, :] = dot(g_ref[some, :], wd_ref[...], 1, 1)
    for b in range(n):
        to = regrouped(b)
        turn_ref[to * per_block : (to + 1) * per_block, :] = raw_ref[b * per_block : (b + 1) * per_block, :]
    for i in range(parts):
        some = slice(i * most, (i + 1) * most)
        d_act = turn_ref[some, :]
        grad = jnp.concatenate([d_act, d_act], axis=1) * cs_ref[some, :]
        d_ref[some, :] = grad
    dr_ref[...] = jnp.zeros_like(dr_ref)
    for b in range(n):
        dm_ref[b * MAIN : (b + 1) * MAIN, :] = d_ref[b * per_block : b * per_block + MAIN, :].astype(BF)
        dr_ref[b * 2 * REM : b * 2 * REM + REM, :] = d_ref[b * per_block + MAIN : (b + 1) * per_block, :]

    tile = 256
    per = 2 * half // copies
    slab = hidden // copies
    base = both * per // 128
    tiles = 2 * half // tile
    turns = 8 * rows // 128
    for j in range(max(tiles, turns)):
        if j < turns:
            some = slice(j * 128, (j + 1) * 128)
            dt_ref[:, some] = d_ref[some, :].astype(BF).T
        if j < tiles:
            down = dot(at_ref[...], g_ref[:, j * tile : (j + 1) * tile]).astype(BF)
            for q in range(tile // 128):
                at = j * tile // 128 + q
                part = down[:, q * 128 : (q + 1) * 128].reshape(copies, slab, 128)
                packed_ref[:, base + at * slab : base + (at + 1) * slab, :] = part
    for j in range(tiles):
        into = dot(dt_ref[...], x_ref[:, j * tile : (j + 1) * tile]).astype(BF)
        for q in range(tile // 128):
            at = j * tile // 128 + q
            owner, piece = at * 128 // per, at % (per // 128)
            packed_ref[owner, piece * both : (piece + 1) * both, :] = into[:, q * 128 : (q + 1) * 128]
    packed_out = pltpu.make_async_copy(packed_ref, packed_hbm, out_sems.at[n])
    packed_out.start()

    sent = []
    parts = 4
    step = n // parts
    most, few = step * MAIN, step * 2 * REM
    for i in range(parts):
        main = dm_ref[i * most : (i + 1) * most, :]
        rest = dr_ref[i * few : (i + 1) * few, :]
        d_left = jnp.concatenate([main, rest.astype(BF)], axis=0)
        d_right = jnp.concatenate([main, pltpu.roll(rest, REM, 0).astype(BF)], axis=0)
        y_left = dot(d_left, wcat_ref[:half, :], 1, 1)
        y_right = dot(d_right, wcat_ref[half:, :], 1, 1)
        some = slice(i * step, (i + 1) * step)
        pair_ref[some, 0:MAIN, :] = y_left[:most].astype(BF).reshape(step, MAIN, half)
        pair_ref[some, MAIN : 2 * MAIN, :] = y_right[:most].astype(BF).reshape(step, MAIN, half)
        tail = (y_left[most:] + y_right[most:]).astype(BF)
        pair_ref[some, 2 * MAIN : PACK, :] = tail.reshape(step, 2 * REM, half)
        for b in range(i * step, (i + 1) * step):
            copy = pltpu.make_async_copy(pair_ref.at[b], pair_hbm.at[to_ref[b]], out_sems.at[b])
            copy.start()
            sent.append(copy)
    for copy in sent:
        copy.wait()
    packed_out.wait()


def middle(to, at_row, gs, xs, wd, wcat, cs, act, copies):
    hidden, width = wd.shape
    both, rows = cs.shape[1], cs.shape[0]
    n, half = to.shape[0], width // 2
    length = 3 * hidden * width // copies // 128
    smem = pl.BlockSpec(memory_space=pltpu.SMEM)
    return pl.pallas_call(
        middle_kernel,
        out_shape=(pltpu.HBM((copies, length, 128), BF), pltpu.HBM((n, PACK, half), BF)),
        in_specs=[smem] * 2 + [pl.BlockSpec(memory_space=pl.ANY)] * 8 + [VMEM] * 5,
        out_specs=(HBM,) * 2,
        scratch_shapes=[
            pltpu.VMEM((rows, width), BF),
            pltpu.VMEM((rows, hidden), F32),
            pltpu.VMEM((rows, hidden), F32),
            pltpu.VMEM((rows, both), F32),
            pltpu.VMEM((both, rows), BF),
            pltpu.VMEM((n * MAIN, both), BF),
            pltpu.VMEM((n * 2 * REM, both), F32),
            pltpu.VMEM((copies, length, 128), BF),
            pltpu.VMEM((n, PACK, half), BF),
            pltpu.SemaphoreType.DMA((8,)),
            pltpu.SemaphoreType.DMA((n + 1,)),
        ],
        compiler_params=pltpu.CompilerParams(vmem_limit_bytes=36 * MIB),
        cost_estimate=pl.CostEstimate(flops=2 * rows * width * 6 * hidden, bytes_accessed=28 * MIB, transcendentals=0),
        name="middle",
    )(to, at_row, *gs, xs, wd, wcat, cs, act)


def unpack_kernel(in_ref, gate_ref, up_ref, down_ref):
    per, hidden = gate_ref.shape
    slab = down_ref.shape[0]
    base = 2 * hidden * per // 128
    for q in range(per // 128):
        both = in_ref[q * 2 * hidden : (q + 1) * 2 * hidden, :].T
        gate_ref[q * 128 : (q + 1) * 128, :] = both[:, :hidden]
        up_ref[q * 128 : (q + 1) * 128, :] = both[:, hidden:]
    for q in range(down_ref.shape[1] // 128):
        down_ref[:, q * 128 : (q + 1) * 128] = in_ref[base + q * slab : base + (q + 1) * slab, :]


def unpack(summed, per, hidden, width, slab):
    vmem = pl.BlockSpec(memory_space=pltpu.VMEM)
    return pl.pallas_call(
        unpack_kernel,
        out_shape=(
            jax.ShapeDtypeStruct((per, hidden), BF),
            jax.ShapeDtypeStruct((per, hidden), BF),
            jax.ShapeDtypeStruct((slab, width), BF),
        ),
        in_specs=[vmem],
        out_specs=(vmem, vmem, vmem),
        cost_estimate=pl.CostEstimate(flops=0, bytes_accessed=2 * MIB, transcendentals=0),
        name="unpack",
    )(summed)


def combine_kernel(ids_ref, ret_ref, out_ref, main_ref, rest_ref):
    experts, _, cols = ret_ref.shape
    toks = out_ref.shape[0]
    half = out_ref.shape[1] // 2
    c = pl.program_id(0)

    @pl.when(c == 0)
    def _():
        pos, _, _ = positions(ids_ref[...], experts)
        main, rest = select(pos)
        left = is_left(*rest.shape)
        main_ref[...] = main.T.astype(BF)
        rest_ref[0] = jnp.where(left, rest, 0.0).T.astype(BF)
        rest_ref[1] = jnp.where(left, 0.0, rest).T.astype(BF)

    tail = ret_ref[:, 2 * MAIN : PACK, :].reshape(experts * 2 * REM, cols)
    for side in range(2):
        body = ret_ref[:, side * MAIN : (side + 1) * MAIN, :].reshape(experts * MAIN, cols)
        total = dot(main_ref[...], body) + dot(rest_ref[side], tail)
        out_ref[:, pl.ds(pl.multiple_of(side * half + c * cols, 128), cols)] = total.astype(BF)


def combine(ids, ret):
    experts, _, half = ret.shape
    toks = ids.shape[1]
    steps = 1
    cols = half // steps
    return pl.pallas_call(
        combine_kernel,
        out_shape=jax.ShapeDtypeStruct((toks, 2 * half), BF),
        grid=(steps,),
        in_specs=[
            pl.BlockSpec(ids.shape, lambda c: (0, 0)),
            pl.BlockSpec((experts, PACK, cols), lambda c: (0, 0, c)),
        ],
        out_specs=pl.BlockSpec((toks, 2 * half), lambda c: (0, 0)),
        scratch_shapes=[
            pltpu.VMEM((toks, experts * MAIN), BF),
            pltpu.VMEM((2, toks, experts * 2 * REM), BF),
        ],
        compiler_params=pltpu.CompilerParams(vmem_limit_bytes=32 * MIB),
        cost_estimate=pl.CostEstimate(flops=2 * 1280 * toks * 2 * half, bytes_accessed=6 * MIB, transcendentals=0),
        name="combine",
    )(ids, ret)


def place(x, y, core):
    return (x % SIDE * SIDE + y % SIDE) * CORES + core


def moved(value, dx, dy, flip):
    if dx == dy == flip == 0:
        return value
    pairs = []
    for x in range(SIDE):
        for y in range(SIDE):
            for core in range(CORES):
                pairs.append((place(x, y, core), place(x + dx, y + dy, core ^ flip)))
    return lax.ppermute(value, "expert", pairs)


def shards(tokens, grad_out, gates, expert_ids, w_gate, w_up, w_down):
    copies = lax.axis_size("dp")
    wg, wu, wd = w_gate[0], w_up[0], w_down[0]
    width, hidden = wg.shape
    me = lax.axis_index("expert")
    x, y, core = me // (SIDE * CORES), me // CORES % SIDE, me % CORES
    wide = lambda values: jnp.broadcast_to(jnp.stack(values).astype(jnp.int32)[:, None], (len(values), 128))
    along_y = wide([place(x, d, f) for d, f in SHIFTS])
    along_x = wide([place(x + d, y, core ^ f) for d, f in SPREAD])
    toks = tokens.shape[0]
    near = jnp.arange(SIDE, dtype=jnp.int32)
    starts_x = near * toks
    starts_g = (y - near + SIDE) % SIDE * toks
    origin = jnp.stack([place(x - d + SIDE, b, f) for b, f in SHIFTS for d in range(SIDE)]).astype(jnp.int32)
    at_row = jnp.stack([(d * CORES + (core ^ f)) * SIDE * (MAIN + REM) for d, f in SPREAD]).astype(jnp.int32)

    ids_t = expert_ids.T
    tokens, grad_out = prepare(ids_t, gates.T, tokens, grad_out)
    near_x, near_g = [tokens], [grad_out]
    for d in (1, SIDE - 1):
        near_x.append(moved(tokens, d, 0, 0))
        near_g.append(moved(grad_out, 0, d, 0))
    cut = toks // 2
    lines_x = [tokens, near_x[1], moved(near_x[1][:cut], 1, 0, 0), moved(near_x[2][cut:], SIDE - 1, 0, 0), near_x[2]]
    lines_g = [grad_out, near_g[1], moved(near_g[1][:cut], 0, 1, 0), moved(near_g[2][cut:], 0, SIDE - 1, 0), near_g[2]]
    lines_x, lines_g = lax.optimization_barrier((lines_x, lines_g))
    (out_x,) = dispatch(along_y, starts_x, lines_x, False)
    columns = [[place(a, b, f) for b in range(SIDE) for f in range(CORES)] for a in range(SIDE)]
    xs = lax.all_to_all(out_x, "expert", split_axis=0, concat_axis=0, axis_index_groups=columns, tiled=True)
    along_x, _ = lax.optimization_barrier((along_x, out_x))
    out_g = dispatch(along_x, starts_g, lines_g, True)
    gs = [moved(v, d, 0, f) for v, (d, f) in zip(out_g, SPREAD)]
    cs, act, wcat, rows_x = forward(xs, wg, wu)
    packed, outgoing = middle(origin, at_row, gs, rows_x, wd, wcat, cs, act, copies)
    summed = lax.psum_scatter(packed, "dp", scatter_dimension=0, tiled=True)[0]
    ret = lax.all_to_all(outgoing, "expert", split_axis=0, concat_axis=0, tiled=True)
    grad_tokens = combine(ids_t, ret)
    grad_g, grad_u, grad_d = unpack(summed, width // copies, hidden, width, hidden // copies)
    return (grad_tokens, grad_g[None], grad_u[None], grad_d[None])


def solution(mesh):
    rows = P(("dp", "expert"), None)
    weights = P("expert", None, None)
    cut = P("expert", "dp", None)
    return jax.shard_map(
        shards,
        mesh=mesh,
        in_specs=(rows, rows, rows, rows, weights, weights, weights),
        out_specs=(rows, cut, cut, cut),
        check_vma=False,
    )
```
